128 devices in a mesh: tm: 16 (over x, y), space: 8 (over z, core).
Axes of the slice: x: 4, y: 4, z: 4, core: 2. Of those that a mesh axis runs over, the one named last changes fastest.
Arguments:
- trajectory: float32 [32, 4, 64, 64, 128], P('tm', None, 'space'), may hold values from -6 to 6
- noise: bfloat16 [32, 4, 64, 64, 128], P('tm', None, 'space'), may hold values from -6 to 6
- timesteps: int32 [33], replicated, may hold values from 0 to 1000, as said below
- w_in: bfloat16 [128, 108], replicated, may hold values from -0.625 to 0.625
- w_time: bfloat16 [128, 128], replicated, may hold values from -0.5 to 0.5
- w_out: bfloat16 [4, 128], replicated, may hold values from -0.5 to 0.5
- well_cells: int32 [8192], P('space'), may hold values from 0 to 65535
- well_owner: int32 [8192, 1], P('space'), may hold values from 0 to 7; in each aligned block of 1024 rows (0 to 1023, 1024 to 2047, ...) at most 512 rows name the same one
- well_values: float32 [8192, 4], P('space'), may hold values from -6 to 6
Outputs:
- states: float32 [32, 4, 64, 64, 128], P('tm', None, 'space')
The draws below stay inside these ranges and needn't reach their ends.
Inputs may be any that keep to these rules, and one draw needn't show every extreme that they name: `timesteps`: strictly falling; the first entry is 1000 and the last 0. `well_cells`: cells are numbered depth first, then the first and the second lateral dimension, within the owning slab. `well_owner`: among the rows of one index of space at most 512 name the same slab, and on some index exactly 512 do.
All inputs are finite; a program needn't handle non-finite values.
Results may differ from the reference program's by a relative error of at most 0.0011.
Values may be sent and summed in bfloat16 or wider, within the bound.
No kernel may reach another device: no remote copies, remote signals or barrier semaphores. Data moves between devices by JAX's collectives and lax.ppermute only.
A program may use at most 192 MiB of HBM per device.

```python
import math
import jax
import jax.numpy as jnp
import numpy as np
from jax import lax

C = 4
HID = 128
TEMB = 128
DEP_DEV = 8
NX = 64
NY = 128
SWEEPS = 2
WROW_DEV = 1024
CAP = 512
SLABS = 8
NDEP = 64
STEPS = 32
WROWS = 8192


def draw_timesteps(key, part):
    shuffled = jax.random.permutation(key, 999).astype(jnp.int32) + 1
    chosen = jnp.sort(shuffled[:STEPS - 1])[::-1]
    return jnp.concatenate([jnp.array([1000], jnp.int32), chosen, jnp.array([0], jnp.int32)]).astype(jnp.int32)


def touch_ends(entries, own_key, least, largest):
    extent = entries.shape
    spot = [jax.random.randint(jax.random.fold_in(own_key, axis), (), 0, extent[axis]) for axis in range(len(extent))]
    entries = entries.at[tuple(spot)].set(least)
    longest = extent.index(max(extent))
    spot[longest] = (spot[longest] + 1) % extent[longest]
    return entries.at[tuple(spot)].set(largest)


def shard_levels(rng, shape, cuts, least, top_value):
    factor_of, own = 1.0, jax.random.fold_in(rng, 6)
    for axis_at, shards_of in cuts:
        heights = jnp.exp(jax.random.uniform(jax.random.fold_in(own, axis_at), (shards_of,), jnp.float32, least / len(cuts), top_value / len(cuts)))
        factor_of = factor_of * jnp.repeat(heights, shape[axis_at] // shards_of).reshape([-1 if axis == axis_at else 1 for axis in range(len(shape))])
    return factor_of


def shared_out(stream_key, own, number, rows, number_of, top, reach, slope):
    ranking = jax.random.permutation(stream_key, number_of)
    heavy_load, usual = portions_of(number_of, rows * top, reach, slope, True), portions_of(number_of, rows * top, reach, slope, False)
    places = jnp.arange(number_of)

    def named(lengths, rotation):
        used = int((lengths > 0).sum())
        fixed = max(1, used // 4)
        moved = fixed + (places - fixed + rotation * (used - fixed)) % max(1, number_of - fixed)
        return jnp.zeros((number_of,), jnp.int32).at[ranking[jnp.where(places < fixed, places, moved)]].set(jnp.asarray(lengths, jnp.int32))

    lengths = jnp.where(number % 4 == 0, named(heavy_load, number // 4), named(usual, number - number // 4 - 1))
    mixed = jax.random.permutation(jax.random.fold_in(own, 3), number_of)
    source_of, taker = mixed[0:number_of // 2 * 2:2], mixed[1:number_of // 2 * 2:2]
    slack = jnp.minimum(lengths[source_of] - 1, reach - lengths[taker]) // 2
    slack = jnp.where((source_of == ranking[0]) | (taker == ranking[0]) | (lengths[taker] == 0), 0, jnp.maximum(slack, 0))
    moved = jax.random.randint(jax.random.fold_in(own, 4), (number_of // 2,), 0, 1 << 20) % (slack + 1)
    lengths = lengths.at[source_of].add(-moved).at[taker].add(moved)
    members = jnp.searchsorted(jnp.cumsum(lengths), jnp.arange(rows * top), side="right").astype(jnp.int32)
    table = members.reshape(top, rows).T
    table = table[jax.random.permutation(jax.random.fold_in(own, 1), rows)]
    rotation = jax.random.randint(jax.random.fold_in(own, 2), (rows, 1), 0, top)
    return jnp.take_along_axis(table, (jnp.arange(top)[None, :] + rotation) % top, axis=1)


def portions_of(count, total, limit, skew, full):
    loads = [(1 << 20) // math.isqrt(grade ** skew) + 1 for grade in range(1, count + 1)]
    largest = limit if full else min(limit, max(-(-total // count), total * loads[0] // sum(loads)))
    least = 1 if total - largest >= count - 1 else 0
    holding, surplus = [largest] + [least] * (count - 1), total - largest - least * (count - 1)
    while surplus > 0:
        movable = [i for i in range(1, count) if holding[i] < largest] or [i for i in range(1, count) if holding[i] < limit]
        whole, budget = sum([loads[i] for i in movable]), surplus
        for i in movable:
            more = min(limit - holding[i], max(1, budget * loads[i] // whole), surplus)
            holding[i] = holding[i] + more
            surplus = surplus - more
    return np.array(holding)


def scatter_about(own_key, dims, deviation, reach, shards=(), kind=jnp.bfloat16):
    values = jax.random.normal(own_key, dims, jnp.float32) * deviation
    if len(shards) > 0:
        values = shard_levels(own_key, dims, shards, -0.22, 0.18) * values
    return jnp.clip(values, min=-reach, max=reach).astype(kind)


def setup_inputs(seed: int = 0) -> dict:
    key_list = jax.random.split(jax.random.key(seed), 10)
    trajectory = scatter_about(key_list[0], (STEPS, C, NDEP, NX, NY), 1.0, 6.0, ((0, 16), (2, 8)), jnp.float32)
    noise = scatter_about(key_list[1], (STEPS, C, NDEP, NX, NY), 1.0, 6.0, ((0, 16), (2, 8)))
    timesteps = draw_timesteps(jax.random.fold_in(key_list[9], 71), 0)
    w_in = scatter_about(key_list[3], (HID, 27 * C), (27 * C) ** -0.5, 0.625)
    w_time = scatter_about(key_list[4], (HID, TEMB), TEMB ** -0.5, 0.5)
    w_out = scatter_about(key_list[5], (C, HID), HID ** -0.5, 0.5)
    well_cells = touch_ends(jax.random.randint(key_list[6], (WROWS,), 0, DEP_DEV * NX * NY), jax.random.fold_in(key_list[6], 1), 0, (DEP_DEV * NX * NY) - 1).astype(jnp.int32)
    well_owner_keys = jax.random.split(jax.random.fold_in(key_list[7], 1), WROWS // WROW_DEV)
    well_owner_turns = jax.random.permutation(jax.random.fold_in(key_list[7], 3), WROWS // WROW_DEV)
    well_owner = jax.vmap(lambda own, number: shared_out(jax.random.fold_in(key_list[7], 2), own, number, WROW_DEV, SLABS, 1, CAP, 2))(well_owner_keys, well_owner_turns).reshape((WROWS, 1))
    well_values = scatter_about(key_list[8], (WROWS, C), 1.0, 6.0, ((0, 8),), jnp.float32)
    return {"trajectory": trajectory, "noise": noise, "timesteps": timesteps, "w_in": w_in, "w_time": w_time, "w_out": w_out, "well_cells": well_cells, "well_owner": well_owner, "well_values": well_values}


GUIDE_GAIN = 2.0
NOISE_COEF = 0.5
TIME_SCALE = 500.0

def conv_drift(padded, w_in, time_bias, w_out):
    channels = padded.shape[0]
    depth_count = padded.shape[1] - 2
    first_len = padded.shape[2] - 2
    second_len = padded.shape[3] - 2

    def one_layer(depth_index):
        slices = lax.dynamic_slice_in_dim(padded, depth_index, 3, 1)
        shifted = [slices[:, depth_off, row_off:row_off + first_len, col_off:col_off + second_len] for depth_off in range(3) for row_off in range(3) for col_off in range(3)]
        patches = jnp.stack(shifted, 0).reshape(27 * channels, first_len * second_len)
        before = jnp.dot(w_in, patches, preferred_element_type=jnp.float32) + time_bias[:, None]
        hidden = jax.nn.silu(before).astype(jnp.bfloat16)
        return jnp.dot(w_out, hidden, preferred_element_type=jnp.float32)
    layers = lax.map(one_layer, jnp.arange(depth_count, dtype=jnp.int32))
    return jnp.transpose(layers, (1, 0, 2)).reshape(channels, depth_count, first_len, second_len)

def time_embed(w_time, time_now):
    half_width = w_time.shape[1] // 2
    frequency = jnp.exp(-math.log(10000.0) * jnp.arange(half_width, dtype=jnp.float32) / half_width)
    angles = time_now.astype(jnp.float32) * frequency
    features = jnp.concatenate([jnp.sin(angles), jnp.cos(angles)]).astype(jnp.bfloat16)
    return jnp.dot(w_time, features, preferred_element_type=jnp.float32)

def increment(state, padded, noise_step, time_now, time_next, w_in, w_time, w_out, observed, well_count):
    step_size = (time_now - time_next).astype(jnp.float32) / TIME_SCALE
    drift = conv_drift(padded, w_in, time_embed(w_time, time_now), w_out)
    drift = drift + GUIDE_GAIN * (observed - well_count * state)
    return step_size * drift + jnp.sqrt(step_size) * NOISE_COEF * noise_step.astype(jnp.float32)

def reference(trajectory, noise, timesteps, w_in, w_time, w_out, well_cells, well_owner, well_values):
    slab_cells = DEP_DEV * NX * NY
    flat_index = well_owner[:, 0].astype(jnp.int32) * slab_cells + well_cells.astype(jnp.int32)
    observed = jnp.zeros((NDEP * NX * NY, C), jnp.float32).at[flat_index].add(well_values)
    observed = jnp.transpose(observed.reshape(NDEP, NX, NY, C), (3, 0, 1, 2))
    well_count = jnp.zeros((NDEP * NX * NY,), jnp.float32).at[flat_index].add(1.0).reshape(NDEP, NX, NY)
    start_state = trajectory[0]
    states = [trajectory[step] for step in range(STEPS)]
    finished = states
    for sweep_index in range(SWEEPS):
        running = start_state
        finished = []
        for step in range(STEPS):
            padded = jnp.pad(states[step].astype(jnp.bfloat16), ((0, 0), (1, 1), (1, 1), (1, 1)))
            running = running + increment(states[step], padded, noise[step], timesteps[step], timesteps[step + 1], w_in, w_time, w_out, observed, well_count)
            finished.append(running)
        states = [start_state] + finished[:-1]
    return jnp.stack(finished)
```

```python
import functools
import math

import jax
import jax.numpy as jnp
import numpy as np
from jax import lax
from jax.experimental import pallas as pl
from jax.experimental.pallas import tpu as pltpu
from jax.sharding import PartitionSpec as P

F32, BF16, I16 = jnp.float32, jnp.bfloat16, jnp.int16
C, HID, ND, NX, NY = 4, 128, 8, 64, 128
TM, SPACE = 16, 8
ROWS = 1024
GUIDE_GAIN = 2.0
NOISE_COEF = 0.5
TIME_SCALE = 500.0
EXP = 16
PAY = 2 * NX + EXP
GPAY = 5 * 32 + EXP
MIB = 2**20


def params(mib):
    return pltpu.CompilerParams(vmem_limit_bytes=mib * MIB)


def smem():
    return pl.BlockSpec(memory_space=pltpu.SMEM)


def full(dims):
    return pl.BlockSpec(dims, lambda i: (0,) * len(dims), pipeline_mode=pl.Buffered(1))


def first_step(v):
    return pl.BlockSpec((1,) + v.shape[1:], lambda i: (0,) * v.ndim, pipeline_mode=pl.Buffered(1))


def call(kernel, name, mib, out_shape, scalars, *args, scratch=(), first=()):
    return pl.pallas_call(
        kernel,
        grid=(1,),
        in_specs=[smem()] * len(scalars) + [first_step(v) if i in first else full(v.shape) for i, v in enumerate(args)],
        out_specs=jax.tree.map(lambda v: full(v.shape), out_shape),
        out_shape=out_shape,
        scratch_shapes=list(scratch),
        compiler_params=params(mib),
        name=name,
    )(*scalars, *args)


def shape(dtype, *dims):
    return jax.ShapeDtypeStruct(dims, dtype)


def selection():
    sel = np.zeros((4, 108, 256), np.float32)
    for xx in range(2):
        for dd in range(2):
            for a in range(3):
                for b in range(3):
                    for e in range(3):
                        for c in range(C):
                            sel[xx * 2 + dd, (9 * a + 3 * b + e) * C + c, (xx + b) * 48 + e * 16 + (dd + a) * 4 + c] = 0.5
    return sel


def pack_kernel(owner_hbm, cell_hbm, value_hbm, traj_hbm, rows_ref, top_ref, bottom_ref, owner, cell, value, first, last, sems):
    copies = [
        pltpu.make_async_copy(src, dst, sems.at[i])
        for i, (src, dst) in enumerate([
            (owner_hbm, owner), (cell_hbm, cell), (value_hbm, value),
            (traj_hbm.at[:, :, 0], first), (traj_hbm.at[:, :, ND - 1], last),
        ])
    ]
    for copy in copies:
        copy.start()
    for copy in copies:
        copy.wait()
    rows = jnp.concatenate(
        [owner[...].astype(F32), cell[...].astype(F32), value[...], jnp.zeros((2, ROWS), F32)], 0
    )
    for k in range(SPACE):
        rows_ref[k] = rows
    top_ref[...] = first[...].astype(BF16)
    bottom_ref[...] = last[...].astype(BF16)


def pack(owner, cells, values, trajectory):
    edge = shape(BF16, 2, C, NX, NY)
    out_shape = [shape(F32, SPACE, 8, ROWS), edge, edge]
    layer = pltpu.VMEM((2, C, NX, NY), F32)
    return pl.pallas_call(
        pack_kernel,
        grid=(1,),
        in_specs=[pl.BlockSpec(memory_space=pltpu.HBM)] * 4,
        out_specs=[full(v.shape) for v in out_shape],
        out_shape=out_shape,
        scratch_shapes=[
            pltpu.VMEM((1, ROWS), jnp.int32), pltpu.VMEM((1, ROWS), jnp.int32), pltpu.VMEM((C, ROWS), F32),
            layer, layer, pltpu.SemaphoreType.DMA((5,)),
        ],
        compiler_params=params(8),
        name="pack",
    )(owner, cells, values, trajectory)


def weights_kernel(rank_ref, w_ref, sel_ref, bias_ref, out_ref, wbig_ref, w2_ref):
    lane = lax.broadcasted_iota(jnp.int32, (HID, 256), 1)
    all_steps = bias_ref[...]
    column = lax.broadcasted_iota(jnp.int32, all_steps.shape, 1)
    extra = []
    for j in range(2):
        b = jnp.sum(jnp.where(column == 2 * rank_ref[0] + j, all_steps, 0.0), axis=1, keepdims=True) * 0.5
        b1 = b.astype(BF16).astype(F32)
        b2 = (b - b1).astype(BF16).astype(F32)
        b3 = b - b1 - b2
        extra.append(jnp.where(lane == 192, b1, jnp.where(lane == 193, b2, jnp.where(lane == 194, b3, 0.0))))
    for k in range(4):
        wk = lax.dot_general(w_ref[...], sel_ref[k], (((0,), (0,)), ((), ())), preferred_element_type=F32)
        for j in range(2):
            wbig_ref[j, k * HID:(k + 1) * HID, :] = (wk + extra[j]).astype(BF16)
    pick = lax.broadcasted_iota(jnp.int32, (16, C), 0) % C == lax.broadcasted_iota(jnp.int32, (16, C), 1)
    tall = jnp.dot(jnp.where(pick, 1.0, 0.0).astype(BF16), out_ref[...], preferred_element_type=F32)
    wide = jnp.concatenate([tall] * 4, 1)
    own = lax.broadcasted_iota(jnp.int32, (16, 512), 0) // C == lax.broadcasted_iota(jnp.int32, (16, 512), 1) // HID
    w2_ref[...] = jnp.where(own, wide, 0.0).astype(BF16)


INNER, OUTER = (1, 2), (0, 3)
CONV_SCRATCH = [
    pltpu.VMEM((NX * 40, NY), F32),
    pltpu.VMEM((2, 66 * 48, NY), BF16),
    pltpu.VMEM((72 * 16, NY), F32),
    pltpu.VMEM((4, 512, 256), BF16),
    pltpu.VMEM((4, 512, 256), BF16),
]


def clear(Q, HB):
    zt = jnp.zeros((48, NY), BF16)
    for i in range(2):
        Q[i, 0:48, :] = zt
        Q[i, 65 * 48:66 * 48, :] = zt
    HB[...] = jnp.zeros(HB.shape, BF16)


def conv_step(layer, pairs, wbig, w2_ref, put, S, Q, So, HA, HB):
    for dp in sorted({2 * p + i for p in pairs for i in range(4)}):
        for c in range(C):
            S[pl.ds(dp * 4 + c, NX, stride=40), :] = layer(c, dp)
    lane = lax.broadcasted_iota(jnp.int32, (16, NY), 1)

    def prep(x, carry):
        base = pl.multiple_of((x + 1) * 48, 16)
        for i, p in enumerate(pairs):
            v = S[pl.ds(pl.multiple_of(x * 40 + 8 * p, 8), 16), :]
            ve = [
                jnp.where(lane == 0, 0.0, pltpu.roll(v, 1, 1)),
                v,
                jnp.where(lane == NY - 1, 0.0, pltpu.roll(v, NY - 1, 1)),
            ]
            for e in range(3):
                Q[i, pl.ds(base + 16 * e, 16), :] = ve[e].astype(BF16)
        return carry

    lax.fori_loop(0, NX, prep, 0, unroll=8)
    ones = jnp.ones((16, 256), BF16)

    def first(t, hidden):
        for g in range(4):
            xq, i = 2 * t + g // 2, g % 2
            b0 = pl.multiple_of(xq * 192, 16)
            pa = Q[i, pl.ds(b0, 192), :]
            pb = Q[i, pl.ds(b0 + 96, 192), :]
            patch = jnp.concatenate([jnp.concatenate([pa, pb], 1), ones], 0)
            u = jnp.dot(wbig[:, 0:208], patch, preferred_element_type=F32)
            hidden[g] = (u + u * jnp.tanh(u)).astype(BF16)
            yield

    def second(t, hidden):
        for g in range(4):
            xq, i = 2 * t + g // 2, g % 2
            r = jnp.dot(w2_ref[...], hidden[g], preferred_element_type=F32)
            for hh in range(2):
                for xx in range(2):
                    st = pl.multiple_of((xq * 4 + 8 + 2 * hh + xx) * 16, 8)
                    So[pl.ds(st + i * 8, 8), :] = r[xx * 8:xx * 8 + 8, hh * NY:hh * NY + NY]
            yield

    def body(i, carry):
        for _ in zip(first(2 * i, HA), second(2 * i - 1, HB)):
            pass
        for _ in zip(first(2 * i + 1, HB), second(2 * i, HA)):
            pass
        return carry

    lax.fori_loop(0, NX // 16, body, 0)
    for _ in second(NX // 8 - 1, HB):
        pass
    for i in range(2):
        for dd in range(2):
            for c in range(C):
                put(c, 2 * i + dd, So[pl.ds(128 + i * 8 + dd * 4 + c, NX, stride=16), :])


def inner(state, wbig, w2_ref, o_ref, scratch):
    clear(scratch[1], scratch[4])
    for j in range(2):
        conv_step(
            lambda c, dp: state(j, c, dp - 1), INNER, wbig.at[j], w2_ref,
            lambda c, i, v: o_ref.__setitem__((j, c, i), v), *scratch,
        )


def outer(state, wbig, w2_ref, lo_ref, hi_ref, o_ref, scratch):
    clear(scratch[1], scratch[4])

    def layer(j, c, dp):
        if dp == 0:
            return lo_ref[j, c].astype(F32)
        if dp == ND + 1:
            return hi_ref[j, c].astype(F32)
        return state(j, c, dp - 1)

    for j in range(2):
        conv_step(
            lambda c, dp: layer(j, c, dp), OUTER, wbig.at[j], w2_ref,
            lambda c, i, v: o_ref.__setitem__((j, c, i), v), *scratch,
        )


def increments(state, rank_ref, ts_ref, in_ref, out_ref, n_ref, g_ref, start, pay_ref, sums_refs):
    tm = rank_ref[0]
    step, gain = [], []
    for j in range(2):
        span = jnp.full((1, NY), ts_ref[2 * tm + j] - ts_ref[2 * tm + j + 1], jnp.int32).astype(F32) / TIME_SCALE
        step.append(span)
        gain.append(jnp.sqrt(span) * NOISE_COEF)
    for p in range(4):
        for c in range(C):
            totals = []
            for dd in range(2):
                d = 2 * p + dd
                observed, count = guide_at(g_ref, d, c)
                total = start(c, d)
                for j in range(2):
                    drift = in_ref[j, c, d - 2] if p in INNER else out_ref[j, c, d if p == 0 else d - 4]
                    drift = drift + GUIDE_GAIN * (observed - count * state(j, c, d))
                    total = total + step[j] * drift + gain[j] * n_ref[j, c, d].astype(F32)
                    if j < len(sums_refs):
                        sums_refs[j][c, d] = total
                totals.append(total)
            encode(totals, lambda at, n, v: pay_ref.__setitem__((c, p, pl.ds(at, n), slice(None)), v))


def given(s_ref):
    return lambda j, c, d: s_ref[j, c, d]


def first_of(rank_ref, start_ref):
    keep = jnp.where(rank_ref[0] == 0, 1.0, 0.0)
    return lambda c, d: keep * start_ref[c, d]


def arrived(e_ref, start, sum_ref):
    def state(j, c, d):
        get = lambda at, n: e_ref[c, d // 2, pl.ds(at, n), :]
        entering = decode(get, d % 2, scale_of(get))
        return entering + (start(c, d) if j == 0 else sum_ref[c, d])

    return state


def inner1_kernel(s_ref, wbig, w2_ref, o_ref, *scratch):
    inner(given(s_ref), wbig, w2_ref, o_ref, scratch)


def inner2_kernel(rank_ref, e_ref, start_ref, sum_ref, wbig, w2_ref, o_ref, *scratch):
    inner(arrived(e_ref, first_of(rank_ref, start_ref.at[0]), sum_ref), wbig, w2_ref, o_ref, scratch)


def outer1_kernel(s_ref, wbig, w2_ref, lo_ref, hi_ref, o_ref, *scratch):
    outer(given(s_ref), wbig, w2_ref, lo_ref, hi_ref, o_ref, scratch)


def increments1_kernel(rank_ref, ts_ref, s_ref, in_ref, out_ref, n_ref, g_ref, pay_ref, sum_ref):
    start = first_of(rank_ref, s_ref.at[0])
    increments(given(s_ref), rank_ref, ts_ref, in_ref, out_ref, n_ref, g_ref, start, pay_ref, [sum_ref])


def outer2_kernel(
    rank_ref, ts_ref, e_ref, traj_ref, before_ref, wbig, w2_ref, lo_ref, hi_ref, in_ref, n_ref, g_ref,
    pay_ref, sum0_ref, sum1_ref, out_ref, *scratch,
):
    start = first_of(rank_ref, traj_ref.at[0])
    state = arrived(e_ref, start, before_ref)
    outer(state, wbig, w2_ref, lo_ref, hi_ref, out_ref, scratch)
    increments(state, rank_ref, ts_ref, in_ref, out_ref, n_ref, g_ref, start, pay_ref, [sum0_ref, sum1_ref])


def edges_kernel(rank_ref, e_ref, start_ref, sum_ref, top_ref, bottom_ref):
    state = arrived(e_ref, first_of(rank_ref, start_ref.at[0]), sum_ref)
    for j in range(2):
        for c in range(C):
            top_ref[j, c] = state(j, c, 0).astype(BF16)
            bottom_ref[j, c] = state(j, c, ND - 1).astype(BF16)


def last_kernel(e_ref, sum0_ref, sum1_ref, o_ref):
    for c in range(C):
        get = lambda at, n: e_ref[c, pl.ds(at, n), :]
        scale = scale_of(get)
        for dd in range(2):
            entering = decode(get, dd, scale)
            o_ref[0, c, dd] = entering + sum0_ref[c, dd]
            o_ref[1, c, dd] = entering + sum1_ref[c, dd]


def last_states(entering, sum0, sum1):
    one = lambda: pl.BlockSpec((C, 2, NX, NY), lambda p: (0, p, 0, 0))
    return pl.pallas_call(
        last_kernel,
        grid=(4,),
        in_specs=[pl.BlockSpec((C, None, PAY, NY), lambda p: (0, p, 0, 0)), one(), one()],
        out_specs=pl.BlockSpec((2, C, 2, NX, NY), lambda p: (0, 0, p, 0, 0)),
        out_shape=shape(F32, 2, C, ND, NX, NY),
        compiler_params=params(16),
        name="last_states",
    )(entering, sum0, sum1)


def wells_kernel(rank_ref, rows_ref, *refs):
    o_ref = refs[-1]
    me_tm, me_space = rank_ref[0], rank_ref[1]
    line = lax.broadcasted_iota(jnp.int32, (32, ROWS), 0) + 32 * me_tm
    column = lax.broadcasted_iota(jnp.int32, (NY, ROWS), 0)
    total = jnp.zeros((13 * 32, NY), F32)
    for src in range(SPACE):
        owner = rows_ref[src, 0:1, :].astype(jnp.int32)
        cell = rows_ref[src, 1:2, :].astype(jnp.int32)
        at_line = jnp.where(owner == me_space, cell >> 7, -1)
        hit = jnp.where(line == at_line, 1.0, 0.0)
        pieces = [hit]
        for c in range(C):
            v = rows_ref[src, 2 + c:3 + c, :]
            v1 = v.astype(BF16).astype(F32)
            v2 = (v - v1).astype(BF16).astype(F32)
            v3 = v - v1 - v2
            pieces += [hit * v1, hit * v2, hit * v3]
        left = jnp.concatenate(pieces, 0).astype(BF16)
        right = jnp.where(column == (cell & 127), 1.0, 0.0).astype(BF16)
        total = total + lax.dot_general(left, right, (((1,), (1,)), ((), ())), preferred_element_type=F32)
    observed = [total[at:at + 32] + total[at + 32:at + 64] + total[at + 64:at + 96] for at in range(32, 13 * 32, 96)]
    power, factor = power_of(observed)
    pieces = [jnp.round(v * factor) for v in observed] + [total[0:32], jnp.broadcast_to(power, (EXP, NY))]
    coded = jnp.concatenate(pieces, 0).astype(jnp.int32).astype(I16)
    for k in range(TM):
        o_ref[k] = coded


def wells(ranks, rows, *earlier):
    return pl.pallas_call(
        wells_kernel,
        grid=(1,),
        in_specs=[smem(), full(rows.shape)] + [pl.BlockSpec(memory_space=pl.ANY)] * len(earlier),
        out_specs=full((TM, GPAY, NY)),
        out_shape=shape(I16, TM, GPAY, NY),
        compiler_params=params(12),
        name="wells",
    )(ranks, rows, *earlier)


def guide_at(g_ref, d, c):
    observed, count = [], []
    for k in (2 * d, 2 * d + 1):
        wide = lambda at, n: g_ref[k, pl.ds(at, n), :].astype(jnp.int32).astype(F32)
        observed.append(wide(c * 32, 32) * jnp.exp2(wide(5 * 32, EXP)[0:1]))
        count.append(wide(4 * 32, 32))
    return jnp.concatenate(observed, 0), jnp.concatenate(count, 0)


def power_of(planes):
    top = functools.reduce(jnp.maximum, [jnp.max(jnp.abs(v), axis=0, keepdims=True) for v in planes])
    power = jnp.ceil(jnp.log2(jnp.maximum(top, 1e-30) * (1.0 / 32000.0)))
    return power, jnp.exp2(-power)


def encode(planes, put):
    power, factor = power_of(planes)
    for i in range(2):
        put(i * NX, NX, jnp.round(planes[i] * factor).astype(jnp.int32).astype(I16))
    put(2 * NX, EXP, jnp.broadcast_to(power, (EXP, NY)).astype(jnp.int32).astype(I16))


def scale_of(get):
    return jnp.exp2(get(2 * NX, EXP).astype(jnp.int32).astype(F32)[0:1])


def decode(get, i, scale):
    return get(i * NX, NX).astype(jnp.int32).astype(F32) * scale


def scan_kernel(got_ref, o_ref):
    running = [jnp.zeros((NX, NY), F32) for _ in range(2)]
    for k in range(TM):
        encode(running, lambda at, n, v: o_ref.__setitem__((k, pl.ds(at, n), slice(None)), v))
        if k < TM - 1:
            get = lambda at, n: got_ref[k, pl.ds(at, n), :]
            scale = scale_of(get)
            running = [running[i] + decode(get, i, scale) for i in range(2)]


def prefix(payload):
    got = lax.all_to_all(payload.reshape(TM, PAY, NY), "tm", 0, 0, tiled=True)
    ahead = call(scan_kernel, "scan", 6, shape(I16, TM, PAY, NY), [], got)
    return lax.all_to_all(ahead, "tm", 0, 0, tiled=True).reshape(C, 4, PAY, NY)


def halos(top, bottom):
    lo = lax.ppermute(bottom, "space", [(i, i + 1) for i in range(SPACE - 1)])
    hi = lax.ppermute(top, "space", [(i + 1, i) for i in range(SPACE - 1)])
    return lo, hi


def time_bias(w_time, times):
    half_width = w_time.shape[1] // 2
    frequency = jnp.exp(-math.log(10000.0) * jnp.arange(half_width, dtype=F32) / half_width)
    angles = times.astype(F32)[None, :] * frequency[:, None]
    features = jnp.concatenate([jnp.sin(angles), jnp.cos(angles)], 0).astype(BF16)
    return jnp.dot(w_time, features, preferred_element_type=F32)


def per_device(trajectory, noise, timesteps, w_in, w_time, w_out, well_cells, well_owner, well_values):
    in_hbm = lambda v: pltpu.with_memory_space_constraint(v, pltpu.HBM)
    trajectory, noise = in_hbm(trajectory), in_hbm(noise)
    ranks = jnp.stack([lax.axis_index("tm"), lax.axis_index("space")]).astype(jnp.int32)
    bias = time_bias(w_time, timesteps[:-1])
    rows, top, bottom = pack(in_hbm(well_owner.T), in_hbm(well_cells[None]), in_hbm(well_values.T), trajectory)
    wbig, w2 = call(
        weights_kernel, "weights", 8, [shape(BF16, 2, 512, 256), shape(BF16, 16, 512)],
        [ranks], w_in.T, jnp.asarray(selection(), BF16), bias, w_out,
    )
    rows = lax.all_to_all(rows, "space", 0, 0, tiled=True)
    lo, hi = halos(top, bottom)

    half = shape(F32, 2, C, 4, NX, NY)
    whole = shape(F32, C, ND, NX, NY)
    coded = shape(I16, C, 4, PAY, NY)
    edge = shape(BF16, 2, C, NX, NY)
    s = trajectory
    part = call(inner1_kernel, "inner1", 20, half, [], s, wbig, w2, scratch=CONV_SCRATCH)
    wbig = in_hbm(wbig)
    guide = wells(ranks, rows, part, lo, hi)
    guide = in_hbm(lax.all_to_all(guide, "tm", 0, 0, tiled=True))
    rest = call(outer1_kernel, "outer1", 20, half, [], s, wbig, w2, lo, hi, scratch=CONV_SCRATCH)
    payload, sums = call(
        increments1_kernel, "increments1", 20, [coded, whole], [ranks, timesteps], s, part, rest, noise, guide
    )
    entering = prefix(payload)
    start = trajectory
    lo, hi = halos(*call(edges_kernel, "edges", 8, [edge, edge], [ranks], entering, start, sums, first=[1]))
    part = call(inner2_kernel, "inner2", 20, half, [ranks], entering, start, sums, wbig, w2, scratch=CONV_SCRATCH, first=[1])
    payload, sum0, sum1 = call(
        outer2_kernel, "outer2", 30, [coded, whole, whole], [ranks, timesteps],
        entering, start, sums, wbig, w2, lo, hi, part, noise, guide, first=[1],
        scratch=[pltpu.VMEM(half.shape, F32)] + CONV_SCRATCH,
    )
    return last_states(prefix(payload), sum0, sum1)


def solution(mesh):
    return jax.shard_map(
        per_device,
        mesh=mesh,
        in_specs=(
            P("tm", None, "space", None, None),
            P("tm", None, "space", None, None),
            P(),
            P(),
            P(),
            P(),
            P("space"),
            P("space", None),
            P("space", None),
        ),
        out_specs=P("tm", None, "space", None, None),
        check_vma=False,
    )
```

```python
import functools
import math

import jax
import jax.numpy as jnp
import numpy as np
from jax import lax
from jax.experimental import pallas as pl
from jax.experimental.pallas import tpu as pltpu
from jax.sharding import PartitionSpec as P

F32, BF16, I16 = jnp.float32, jnp.bfloat16, jnp.int16
C, HID, ND, NX, NY = 4, 128, 8, 64, 128
TM, SPACE = 16, 8
ROWS = 1024
GUIDE_GAIN = 2.0
NOISE_COEF = 0.5
TIME_SCALE = 500.0
EXP = 8
PAY = 2 * NX + EXP
GPAY = 5 * 32 + 16
MIB = 2**20


def params(mib):
    return pltpu.CompilerParams(vmem_limit_bytes=mib * MIB)


def smem():
    return pl.BlockSpec(memory_space=pltpu.SMEM)


def full(dims):
    return pl.BlockSpec(dims, lambda i: (0,) * len(dims), pipeline_mode=pl.Buffered(1))


def in_hbm(value):
    return pltpu.with_memory_space_constraint(value, pltpu.HBM)


class Hbm:
    def __init__(self, value):
        self.value = in_hbm(value)


class Anywhere:
    def __init__(self, value):
        self.value = value


class First:
    def __init__(self, value):
        self.value = in_hbm(value)


def spec_of(v):
    if isinstance(v, Hbm):
        return pl.BlockSpec(memory_space=pltpu.HBM)
    if isinstance(v, Anywhere):
        return pl.BlockSpec(memory_space=pl.ANY)
    if isinstance(v, First):
        dims = v.value.shape
        return pl.BlockSpec((1,) + dims[1:], lambda i: (0,) * len(dims), pipeline_mode=pl.Buffered(1))
    return full(v.shape)


def call(kernel, name, mib, out_shape, scalars, *args, scratch=()):
    return pl.pallas_call(
        kernel,
        grid=(1,),
        in_specs=[smem()] * len(scalars) + [spec_of(v) for v in args],
        out_specs=jax.tree.map(lambda v: full(v.shape), out_shape),
        out_shape=out_shape,
        scratch_shapes=list(scratch),
        compiler_params=params(mib),
        name=name,
    )(*scalars, *[v.value if isinstance(v, (Hbm, Anywhere, First)) else v for v in args])


class Loads:
    def __init__(self, sems, **groups):
        self.copies, at = {}, 0
        for name, pairs in groups.items():
            self.copies[name] = [pltpu.make_async_copy(src, dst, sems.at[at + i]) for i, (src, dst) in enumerate(pairs)]
            at += len(pairs)
        for copies in self.copies.values():
            for copy in copies:
                copy.start()

    def wait(self, name):
        for copy in self.copies.pop(name, []):
            copy.wait()


def shape(dtype, *dims):
    return jax.ShapeDtypeStruct(dims, dtype)


def selection():
    sel = np.zeros((4, 108, 256), np.float32)
    for xx in range(2):
        for dd in range(2):
            for a in range(3):
                for b in range(3):
                    for e in range(3):
                        for c in range(C):
                            sel[xx * 2 + dd, (9 * a + 3 * b + e) * C + c, (xx + b) * 48 + e * 16 + (dd + a) * 4 + c] = 0.5
    return sel


def pack_kernel(owner_hbm, cell_hbm, value_hbm, traj_hbm, rows_ref, top_ref, bottom_ref, owner, cell, value, first, last, sems):
    copies = [
        pltpu.make_async_copy(src, dst, sems.at[i])
        for i, (src, dst) in enumerate([
            (owner_hbm, owner), (cell_hbm, cell), (value_hbm, value),
            (traj_hbm.at[:, :, 0], first), (traj_hbm.at[:, :, ND - 1], last),
        ])
    ]
    for copy in copies:
        copy.start()
    for copy in copies:
        copy.wait()
    rows = jnp.concatenate(
        [owner[...].astype(F32), cell[...].astype(F32), value[...], jnp.zeros((2, ROWS), F32)], 0
    )
    for k in range(SPACE):
        rows_ref[k] = rows
    top_ref[...] = first[...].astype(BF16)
    bottom_ref[...] = last[...].astype(BF16)


def pack(owner, cells, values, trajectory):
    edge = shape(BF16, 2, C, NX, NY)
    out_shape = [shape(F32, SPACE, 8, ROWS), edge, edge]
    layer = pltpu.VMEM((2, C, NX, NY), F32)
    return pl.pallas_call(
        pack_kernel,
        grid=(1,),
        in_specs=[pl.BlockSpec(memory_space=pltpu.HBM)] * 4,
        out_specs=[full(v.shape) for v in out_shape],
        out_shape=out_shape,
        scratch_shapes=[
            pltpu.VMEM((1, ROWS), jnp.int32), pltpu.VMEM((1, ROWS), jnp.int32), pltpu.VMEM((C, ROWS), F32),
            layer, layer, pltpu.SemaphoreType.DMA((5,)),
        ],
        compiler_params=params(8),
        name="pack",
    )(owner, cells, values, trajectory)


def weights_kernel(rank_ref, w_ref, sel_ref, bias_ref, out_ref, wbig_ref, w2_ref):
    lane = lax.broadcasted_iota(jnp.int32, (HID, 256), 1)
    all_steps = bias_ref[...]
    column = lax.broadcasted_iota(jnp.int32, all_steps.shape, 1)
    extra = []
    for j in range(2):
        b = jnp.sum(jnp.where(column == 2 * rank_ref[0] + j, all_steps, 0.0), axis=1, keepdims=True) * 0.5
        b1 = b.astype(BF16).astype(F32)
        b2 = (b - b1).astype(BF16).astype(F32)
        b3 = b - b1 - b2
        extra.append(jnp.where(lane == 192, b1, jnp.where(lane == 193, b2, jnp.where(lane == 194, b3, 0.0))))
    for k in range(4):
        wk = lax.dot_general(w_ref[...], sel_ref[k], (((0,), (0,)), ((), ())), preferred_element_type=F32)
        for j in range(2):
            wbig_ref[j, k * HID:(k + 1) * HID, :] = (wk + extra[j]).astype(BF16)
    pick = lax.broadcasted_iota(jnp.int32, (16, C), 0) % C == lax.broadcasted_iota(jnp.int32, (16, C), 1)
    tall = jnp.dot(jnp.where(pick, 1.0, 0.0).astype(BF16), out_ref[...], preferred_element_type=F32)
    wide = jnp.concatenate([tall] * 4, 1)
    own = lax.broadcasted_iota(jnp.int32, (16, 512), 0) // C == lax.broadcasted_iota(jnp.int32, (16, 512), 1) // HID
    w2_ref[...] = jnp.where(own, wide, 0.0).astype(BF16)


INNER, OUTER = (1, 2), (0, 3)
CONV_SCRATCH = [
    pltpu.VMEM((2, 512, 256), BF16),
    pltpu.VMEM(((NX + 9) * 40, NY), F32),
    pltpu.VMEM((2, (NX + 10) * 48, NY), BF16),
    pltpu.VMEM((72 * 16, NY), F32),
    pltpu.VMEM((4, 512, 256), BF16),
    pltpu.VMEM((4, 512, 256), BF16),
]


def clear(S, Q, HB):
    S[NX * 40:(NX + 9) * 40, :] = jnp.zeros((9 * 40, NY), F32)
    for i in range(2):
        Q[i, 0:48, :] = jnp.zeros((48, NY), BF16)
    HB[...] = jnp.zeros(HB.shape, BF16)


def conv_step(layer, pairs, wbig, w2_ref, put, S, Q, So, HA, HB, ready):
    for dp in sorted({2 * p + i for p in pairs for i in range(4)}):
        for c in range(C):
            S[pl.ds(dp * 4 + c, NX, stride=40), :] = layer(c, dp)
    lane = lax.broadcasted_iota(jnp.int32, (16, NY), 1)

    def prep(x):
        base = pl.multiple_of((x + 1) * 48, 16)
        for i, p in enumerate(pairs):
            v = S[pl.ds(pl.multiple_of(x * 40 + 8 * p, 8), 16), :]
            ve = [
                jnp.where(lane == 0, 0.0, pltpu.roll(v, 1, 1)),
                v,
                jnp.where(lane == NY - 1, 0.0, pltpu.roll(v, NY - 1, 1)),
            ]
            for e in range(3):
                Q[i, pl.ds(base + 16 * e, 16), :] = ve[e].astype(BF16)

    for x in range(9):
        prep(x)
    ready()
    ones = jnp.ones((16, 256), BF16)

    def first(t, hidden):
        for g in range(4):
            xq, i = 2 * t + g // 2, g % 2
            b0 = pl.multiple_of(xq * 192, 16)
            pa = Q[i, pl.ds(b0, 192), :]
            pb = Q[i, pl.ds(b0 + 96, 192), :]
            patch = jnp.concatenate([jnp.concatenate([pa, pb], 1), ones], 0)
            u = jnp.dot(wbig[:, 0:208], patch, preferred_element_type=F32)
            hidden[g] = (u + u * jnp.tanh(u)).astype(BF16)
            for k in range(2):
                prep(8 * t + 9 + 2 * g + k)
            yield

    def second(t, hidden):
        for g in range(4):
            xq, i = 2 * t + g // 2, g % 2
            r = jnp.dot(w2_ref[...], hidden[g], preferred_element_type=F32)
            for hh in range(2):
                for xx in range(2):
                    st = pl.multiple_of((xq * 4 + 8 + 2 * hh + xx) * 16, 8)
                    So[pl.ds(st + i * 8, 8), :] = r[xx * 8:xx * 8 + 8, hh * NY:hh * NY + NY]
            yield

    def body(i, carry):
        for _ in zip(first(2 * i, HA), second(2 * i - 1, HB)):
            pass
        for _ in zip(first(2 * i + 1, HB), second(2 * i, HA)):
            pass
        return carry

    lax.fori_loop(0, NX // 16, body, 0)
    for _ in second(NX // 8 - 1, HB):
        pass
    for i in range(2):
        for dd in range(2):
            for c in range(C):
                put(c, 2 * i + dd, So[pl.ds(128 + i * 8 + dd * 4 + c, NX, stride=16), :])


def convolve(state, pairs, halo, w2_ref, put, loads, scratch):
    wbig, S, Q, So, HA, HB = scratch
    clear(S, Q, HB)

    def layer(j, c, dp):
        if dp in (0, ND + 1):
            return halo[dp > 0][j, c].astype(F32)
        return state(j, c, dp - 1)

    for j in range(2):
        loads.wait(f"step{j}")
        conv_step(
            lambda c, dp: layer(j, c, dp), pairs, wbig.at[j], w2_ref, lambda c, i, v: put(j, c, i, v),
            S, Q, So, HA, HB, lambda: loads.wait("weights"),
        )


def increments(state, rank_ref, ts_ref, in_ref, out_ref, n_ref, g_ref, start, pay_ref, sums_refs):
    step, gain = gains(rank_ref, ts_ref)
    for p in range(4):
        for c in range(C):
            totals = []
            for dd in range(2):
                d = 2 * p + dd
                observed, count = guide_at(g_ref, d, c)
                total = start(c, d)
                for j in range(2):
                    drift = in_ref[j, c, d - 2] if p in INNER else out_ref[j, c, d if p == 0 else d - 4]
                    drift = drift + GUIDE_GAIN * (observed - count * state(j, c, d))
                    total = total + step[j] * drift + gain[j] * n_ref[j, c, d].astype(F32)
                    if j < len(sums_refs):
                        sums_refs[j][c, d] = total
                totals.append(total)
            encode(totals, lambda at, n, v: pay_ref.__setitem__((c, p, pl.ds(at, n), slice(None)), v))


def given(s_ref):
    return lambda j, c, d: s_ref[j, c, d]


def first_of(rank_ref, start_ref):
    keep = jnp.where(rank_ref[0] == 0, 1.0, 0.0)
    return lambda c, d: keep * start_ref[c, d]


def arrived(e_ref, start, sum_ref):
    def state(j, c, d):
        get = lambda at, n: e_ref[c, d // 2, pl.ds(at, n), :]
        entering = decode(get, d % 2, scale_of(get))
        return entering + (start(c, d) if j == 0 else sum_ref[c, d])

    return state


def inner1_kernel(s_hbm, wbig_hbm, w2_ref, o_ref, s, sems, *scratch):
    loads = Loads(
        sems, step0=[(s_hbm.at[0, :, 1:7], s.at[0])], weights=[(wbig_hbm, scratch[0])], step1=[(s_hbm.at[1, :, 1:7], s.at[1])]
    )
    put = lambda j, c, i, v: o_ref.__setitem__((j, c, i), v)
    convolve(lambda j, c, d: s[j, c, d - 1], INNER, None, w2_ref, put, loads, scratch)


def outer1_kernel(s_hbm, wbig_hbm, w2_ref, lo_ref, hi_ref, o_ref, s, sems, *scratch):
    step = lambda j: [(s_hbm.at[j, :, 0:3], s.at[j, :, 0:3]), (s_hbm.at[j, :, 5:8], s.at[j, :, 3:6])]
    loads = Loads(sems, step0=step(0), weights=[(wbig_hbm, scratch[0])], step1=step(1))
    put = lambda j, c, i, v: o_ref.__setitem__((j, c, i), v)
    state = lambda j, c, d: s[j, c, d if d < 3 else d - 2]
    convolve(state, OUTER, (lo_ref, hi_ref), w2_ref, put, loads, scratch)


def gains(rank_ref, ts_ref):
    tm = rank_ref[0]
    step, gain = [], []
    for j in range(2):
        span = jnp.full((1, NY), ts_ref[2 * tm + j] - ts_ref[2 * tm + j + 1], jnp.int32).astype(F32) / TIME_SCALE
        step.append(span)
        gain.append(jnp.sqrt(span) * NOISE_COEF)
    return step, gain


def increments1_kernel(rank_ref, ts_ref, s_ref, in_ref, out_ref, n_ref, g_ref, pay_ref, sum_ref):
    step, gain = gains(rank_ref, ts_ref)
    keep = jnp.where(rank_ref[0] == 0, 1.0, 0.0)
    pair = pl.program_id(0)
    is_inner = jnp.logical_or(pair == 1, pair == 2)
    for c in range(C):
        totals = []
        for dd in range(2):
            observed, count = guide_at(g_ref, dd, c)
            total = keep * s_ref[0, c, dd]
            for j in range(2):
                drift = jnp.where(is_inner, in_ref[j, c, dd], out_ref[j, c, dd])
                drift = drift + GUIDE_GAIN * (observed - count * s_ref[j, c, dd])
                total = total + step[j] * drift + gain[j] * n_ref[j, c, dd].astype(F32)
                if j == 0:
                    sum_ref[c, dd] = total
            totals.append(total)
        encode(totals, lambda at, n, v: pay_ref.__setitem__((c, pl.ds(at, n), slice(None)), v))


def increments1(ranks, timesteps, s, inner, outer, noise, guide):
    pair = lambda place: pl.BlockSpec((2, C, 2, NX, NY), lambda p: (0, 0, place(p), 0, 0))
    return pl.pallas_call(
        increments1_kernel,
        grid=(4,),
        in_specs=[
            smem(), smem(), pair(lambda p: p), pair(lambda p: p // 2), pair(lambda p: p // 2), pair(lambda p: p),
            pl.BlockSpec((4, GPAY, NY), lambda p: (p, 0, 0)),
        ],
        out_specs=[
            pl.BlockSpec((C, None, PAY, NY), lambda p: (0, p, 0, 0)),
            pl.BlockSpec((C, 2, NX, NY), lambda p: (0, p, 0, 0)),
        ],
        out_shape=[shape(I16, C, 4, PAY, NY), shape(F32, C, ND, NX, NY)],
        compiler_params=params(16),
        name="increments1",
    )(ranks, timesteps, s, inner, outer, noise, guide)


def inner2_kernel(rank_ref, e_ref, traj_hbm, before_hbm, wbig_hbm, w2_ref, o_ref, traj, before, sems, *scratch):
    loads = Loads(
        sems, step0=[(traj_hbm.at[0, :, 1:7], traj.at[0, :, 1:7])], weights=[(wbig_hbm, scratch[0])],
        step1=[(before_hbm.at[:, 1:7], before.at[:, 1:7])],
    )
    state = arrived(e_ref, first_of(rank_ref, traj.at[0]), before)
    put = lambda j, c, i, v: o_ref.__setitem__((j, c, i), v)
    convolve(state, INNER, None, w2_ref, put, loads, scratch)


def outer2_kernel(
    rank_ref, ts_ref, e_ref, lo_ref, hi_ref, w2_ref, traj_hbm, before_hbm, wbig_hbm, in_hbm_ref, n_hbm, g_hbm,
    pay_ref, sum0_ref, sum1_ref, traj, before, in_ref, n_ref, g_ref, out_ref, sems, *scratch,
):
    loads = Loads(
        sems, step0=[(traj_hbm.at[0:1], traj)], weights=[(wbig_hbm, scratch[0])], step1=[(before_hbm, before)],
        late=[(n_hbm, n_ref), (g_hbm, g_ref), (in_hbm_ref, in_ref)],
    )
    start = first_of(rank_ref, traj.at[0])
    state = arrived(e_ref, start, before)
    put = lambda j, c, i, v: out_ref.__setitem__((j, c, i), v)
    convolve(state, OUTER, (lo_ref, hi_ref), w2_ref, put, loads, scratch)
    loads.wait("late")
    increments(state, rank_ref, ts_ref, in_ref, out_ref, n_ref, g_ref, start, pay_ref, [sum0_ref, sum1_ref])


def edges_kernel(rank_ref, e_ref, start_ref, sum_ref, top_ref, bottom_ref):
    state = arrived(e_ref, first_of(rank_ref, start_ref.at[0]), sum_ref)
    for j in range(2):
        for c in range(C):
            top_ref[j, c] = state(j, c, 0).astype(BF16)
            bottom_ref[j, c] = state(j, c, ND - 1).astype(BF16)


def last_kernel(e_ref, sum0_ref, sum1_ref, o_ref):
    for c in range(C):
        get = lambda at, n: e_ref[c, pl.ds(at, n), :]
        scale = scale_of(get)
        for dd in range(2):
            entering = decode(get, dd, scale)
            o_ref[0, c, dd] = entering + sum0_ref[c, dd]
            o_ref[1, c, dd] = entering + sum1_ref[c, dd]


def last_states(entering, sum0, sum1):
    one = lambda: pl.BlockSpec((C, 2, NX, NY), lambda p: (0, p, 0, 0))
    return pl.pallas_call(
        last_kernel,
        grid=(4,),
        in_specs=[pl.BlockSpec((C, None, PAY, NY), lambda p: (0, p, 0, 0)), one(), one()],
        out_specs=pl.BlockSpec((2, C, 2, NX, NY), lambda p: (0, 0, p, 0, 0)),
        out_shape=shape(F32, 2, C, ND, NX, NY),
        compiler_params=params(16),
        name="last_states",
    )(entering, sum0, sum1)


def wells_kernel(rank_ref, rows_ref, *refs):
    o_ref = refs[-1]
    me_tm, me_space = rank_ref[0], rank_ref[1]
    line = lax.broadcasted_iota(jnp.int32, (32, ROWS), 0) + 32 * me_tm
    column = lax.broadcasted_iota(jnp.int32, (NY, ROWS), 0)
    total = jnp.zeros((13 * 32, NY), F32)
    for src in range(SPACE):
        owner = rows_ref[src, 0:1, :].astype(jnp.int32)
        cell = rows_ref[src, 1:2, :].astype(jnp.int32)
        at_line = jnp.where(owner == me_space, cell >> 7, -1)
        hit = jnp.where(line == at_line, 1.0, 0.0)
        pieces = [hit]
        for c in range(C):
            v = rows_ref[src, 2 + c:3 + c, :]
            v1 = v.astype(BF16).astype(F32)
            v2 = (v - v1).astype(BF16).astype(F32)
            v3 = v - v1 - v2
            pieces += [hit * v1, hit * v2, hit * v3]
        left = jnp.concatenate(pieces, 0).astype(BF16)
        right = jnp.where(column == (cell & 127), 1.0, 0.0).astype(BF16)
        total = total + lax.dot_general(left, right, (((1,), (1,)), ((), ())), preferred_element_type=F32)
    observed = [total[at:at + 32] + total[at + 32:at + 64] + total[at + 64:at + 96] for at in range(32, 13 * 32, 96)]
    power, factor = power_of(observed)
    pieces = [jnp.round(v * factor) for v in observed] + [total[0:32], jnp.broadcast_to(power, (16, NY))]
    coded = jnp.concatenate(pieces, 0).astype(jnp.int32).astype(I16)
    for k in range(TM):
        o_ref[k] = coded


def wells(ranks, rows, *earlier):
    return pl.pallas_call(
        wells_kernel,
        grid=(1,),
        in_specs=[smem(), full(rows.shape)] + [pl.BlockSpec(memory_space=pl.ANY)] * len(earlier),
        out_specs=full((TM, GPAY, NY)),
        out_shape=shape(I16, TM, GPAY, NY),
        compiler_params=params(12),
        name="wells",
    )(ranks, rows, *earlier)


def guide_at(g_ref, d, c):
    observed, count = [], []
    for k in (2 * d, 2 * d + 1):
        wide = lambda at, n: g_ref[k, pl.ds(at, n), :].astype(jnp.int32).astype(F32)
        observed.append(wide(c * 32, 32) * jnp.exp2(wide(5 * 32, 16)[0:1]))
        count.append(wide(4 * 32, 32))
    return jnp.concatenate(observed, 0), jnp.concatenate(count, 0)


def power_of(planes):
    top = functools.reduce(jnp.maximum, [jnp.max(jnp.abs(v), axis=0, keepdims=True) for v in planes])
    power = jnp.ceil(jnp.log2(jnp.maximum(top, 1e-30) * (1.0 / 32000.0)))
    return power, jnp.exp2(-power)


def encode(planes, put):
    power, factor = power_of(planes)
    for i in range(2):
        put(i * NX, NX, jnp.round(planes[i] * factor).astype(jnp.int32).astype(I16))
    put(2 * NX, EXP, jnp.broadcast_to(power, (EXP, NY)).astype(jnp.int32).astype(I16))


def scale_of(get):
    return jnp.exp2(get(2 * NX, EXP).astype(jnp.int32).astype(F32)[0:1])


def decode(get, i, scale):
    return get(i * NX, NX).astype(jnp.int32).astype(F32) * scale


def scan_kernel(got_ref, o_ref):
    running = [jnp.zeros((NX, NY), F32) for _ in range(2)]
    for k in range(TM):
        encode(running, lambda at, n, v: o_ref.__setitem__((k, pl.ds(at, n), slice(None)), v))
        if k < TM - 1:
            get = lambda at, n: got_ref[k, pl.ds(at, n), :]
            scale = scale_of(get)
            running = [running[i] + decode(get, i, scale) for i in range(2)]


def prefix(payload):
    got = lax.all_to_all(payload.reshape(TM, PAY, NY), "tm", 0, 0, tiled=True)
    ahead = call(scan_kernel, "scan", 6, shape(I16, TM, PAY, NY), [], got)
    return lax.all_to_all(ahead, "tm", 0, 0, tiled=True).reshape(C, 4, PAY, NY)


def halos(top, bottom):
    lo = lax.ppermute(bottom, "space", [(i, i + 1) for i in range(SPACE - 1)])
    hi = lax.ppermute(top, "space", [(i + 1, i) for i in range(SPACE - 1)])
    return lo, hi


def time_bias(w_time, times):
    half_width = w_time.shape[1] // 2
    frequency = jnp.exp(-math.log(10000.0) * jnp.arange(half_width, dtype=F32) / half_width)
    angles = times.astype(F32)[None, :] * frequency[:, None]
    features = jnp.concatenate([jnp.sin(angles), jnp.cos(angles)], 0).astype(BF16)
    return jnp.dot(w_time, features, preferred_element_type=F32)


def per_device(trajectory, noise, timesteps, w_in, w_time, w_out, well_cells, well_owner, well_values):
    ranks = jnp.stack([lax.axis_index("tm"), lax.axis_index("space")]).astype(jnp.int32)
    bias = time_bias(w_time, timesteps[:-1])
    rows, top, bottom = pack(in_hbm(well_owner.T), in_hbm(well_cells[None]), in_hbm(well_values.T), in_hbm(trajectory))
    wbig, w2 = call(
        weights_kernel, "weights", 8, [shape(BF16, 2, 512, 256), shape(BF16, 16, 512)],
        [ranks], w_in.T, jnp.asarray(selection(), BF16), bias, w_out,
    )
    rows = lax.all_to_all(rows, "space", 0, 0, tiled=True)
    lo, hi = halos(top, bottom)

    half = shape(F32, 2, C, 4, NX, NY)
    whole = shape(F32, C, ND, NX, NY)
    coded = shape(I16, C, 4, PAY, NY)
    edge = shape(BF16, 2, C, NX, NY)
    vm = lambda *dims: pltpu.VMEM(dims, F32)
    six = vm(2, C, 6, NX, NY)
    sems = lambda n: pltpu.SemaphoreType.DMA((n,))
    s, wbig = Hbm(trajectory), Anywhere(wbig)
    part = call(inner1_kernel, "inner1", 20, half, [], s, wbig, w2, scratch=[six, sems(3)] + CONV_SCRATCH)
    guide = wells(ranks, rows, part, lo, hi)
    guide = lax.all_to_all(guide, "tm", 0, 0, tiled=True)
    rest = call(outer1_kernel, "outer1", 20, half, [], s, wbig, w2, lo, hi, scratch=[six, sems(5)] + CONV_SCRATCH)
    payload, sums = increments1(ranks, timesteps, s.value, part, rest, in_hbm(noise), guide)
    entering = prefix(payload)
    lo, hi = halos(*call(edges_kernel, "edges", 8, [edge, edge], [ranks], entering, First(trajectory), sums))
    sums = Anywhere(sums)
    part = call(
        inner2_kernel, "inner2", 20, half, [ranks], entering, s, sums, wbig, w2,
        scratch=[vm(1, C, ND, NX, NY), vm(C, ND, NX, NY), sems(3)] + CONV_SCRATCH,
    )
    payload, sum0, sum1 = call(
        outer2_kernel, "outer2", 32, [coded, whole, whole], [ranks, timesteps],
        entering, lo, hi, w2, s, sums, wbig, Anywhere(part), Hbm(noise), Anywhere(guide),
        scratch=[
            vm(1, C, ND, NX, NY), vm(C, ND, NX, NY), vm(*half.shape), pltpu.VMEM((2, C, ND, NX, NY), BF16),
            pltpu.VMEM((TM, GPAY, NY), I16), vm(*half.shape), sems(6),
        ] + CONV_SCRATCH,
    )
    return last_states(prefix(payload), sum0, sum1)


def solution(mesh):
    return jax.shard_map(
        per_device,
        mesh=mesh,
        in_specs=(
            P("tm", None, "space", None, None),
            P("tm", None, "space", None, None),
            P(),
            P(),
            P(),
            P(),
            P("space"),
            P("space", None),
            P("space", None),
        ),
        out_specs=P("tm", None, "space", None, None),
        check_vma=False,
    )
```

```python
import functools
import math

import jax
import jax.numpy as jnp
import numpy as np
from jax import lax
from jax.experimental import pallas as pl
from jax.experimental.pallas import tpu as pltpu
from jax.sharding import PartitionSpec as P

F32, BF16, I16 = jnp.float32, jnp.bfloat16, jnp.int16
C, HID, ND, NX, NY = 4, 128, 8, 64, 128
TM, SPACE = 16, 8
ROWS = 1024
GUIDE_GAIN = 2.0
NOISE_COEF = 0.5
TIME_SCALE = 500.0
EXP = 8
PAY = 2 * NX + EXP
GROWS = 5 * NX + 16
MIB = 2**20


def params(mib):
    return pltpu.CompilerParams(vmem_limit_bytes=mib * MIB)


def smem():
    return pl.BlockSpec(memory_space=pltpu.SMEM)


def full(dims):
    return pl.BlockSpec(dims, lambda i: (0,) * len(dims), pipeline_mode=pl.Buffered(1))


def in_hbm(value):
    return pltpu.with_memory_space_constraint(value, pltpu.HBM)


class Hbm:
    def __init__(self, value):
        self.value = in_hbm(value)


class Anywhere:
    def __init__(self, value):
        self.value = value


class First:
    def __init__(self, value):
        self.value = in_hbm(value)


def spec_of(v):
    if isinstance(v, Hbm):
        return pl.BlockSpec(memory_space=pltpu.HBM)
    if isinstance(v, Anywhere):
        return pl.BlockSpec(memory_space=pl.ANY)
    if isinstance(v, First):
        dims = v.value.shape
        return pl.BlockSpec((1,) + dims[1:], lambda i: (0,) * len(dims), pipeline_mode=pl.Buffered(1))
    return full(v.shape)


def call(kernel, name, mib, out_shape, scalars, *args, scratch=()):
    return pl.pallas_call(
        kernel,
        grid=(1,),
        in_specs=[smem()] * len(scalars) + [spec_of(v) for v in args],
        out_specs=jax.tree.map(lambda v: full(v.shape), out_shape),
        out_shape=out_shape,
        scratch_shapes=list(scratch),
        compiler_params=params(mib),
        name=name,
    )(*scalars, *[v.value if isinstance(v, (Hbm, Anywhere, First)) else v for v in args])


class Loads:
    def __init__(self, sems, **groups):
        self.copies, at = {}, 0
        for name, pairs in groups.items():
            self.copies[name] = [pltpu.make_async_copy(src, dst, sems.at[at + i]) for i, (src, dst) in enumerate(pairs)]
            at += len(pairs)
        for copies in self.copies.values():
            for copy in copies:
                copy.start()

    def wait(self, name):
        for copy in self.copies.pop(name, []):
            copy.wait()


def shape(dtype, *dims):
    return jax.ShapeDtypeStruct(dims, dtype)


def selection():
    sel = np.zeros((4, 108, 256), np.float32)
    for xx in range(2):
        for dd in range(2):
            for a in range(3):
                for b in range(3):
                    for e in range(3):
                        for c in range(C):
                            sel[xx * 2 + dd, (9 * a + 3 * b + e) * C + c, (xx + b) * 48 + e * 16 + (dd + a) * 4 + c] = 0.5
    return sel


def pack_kernel(owner_hbm, cell_hbm, value_hbm, traj_hbm, rows_ref, top_ref, bottom_ref, owner, cell, value, first, last, sems):
    copies = [
        pltpu.make_async_copy(src, dst, sems.at[i])
        for i, (src, dst) in enumerate([
            (owner_hbm, owner), (cell_hbm, cell), (value_hbm, value),
            (traj_hbm.at[:, :, 0], first), (traj_hbm.at[:, :, ND - 1], last),
        ])
    ]
    for copy in copies:
        copy.start()
    for copy in copies:
        copy.wait()
    rows = jnp.concatenate(
        [owner[...].astype(F32), cell[...].astype(F32), value[...], jnp.zeros((2, ROWS), F32)], 0
    )
    for k in range(SPACE):
        rows_ref[k] = rows
    top_ref[...] = first[...].astype(BF16)
    bottom_ref[...] = last[...].astype(BF16)


def pack(owner, cells, values, trajectory):
    edge = shape(BF16, 2, C, NX, NY)
    out_shape = [shape(F32, SPACE, 8, ROWS), edge, edge]
    layer = pltpu.VMEM((2, C, NX, NY), F32)
    return pl.pallas_call(
        pack_kernel,
        grid=(1,),
        in_specs=[pl.BlockSpec(memory_space=pltpu.HBM)] * 4,
        out_specs=[full(v.shape) for v in out_shape],
        out_shape=out_shape,
        scratch_shapes=[
            pltpu.VMEM((1, ROWS), jnp.int32), pltpu.VMEM((1, ROWS), jnp.int32), pltpu.VMEM((C, ROWS), F32),
            layer, layer, pltpu.SemaphoreType.DMA((5,)),
        ],
        compiler_params=params(8),
        name="pack",
    )(owner, cells, values, trajectory)


def weights_kernel(rank_ref, w_ref, sel_ref, bias_ref, out_ref, wbig_ref, w2_ref):
    lane = lax.broadcasted_iota(jnp.int32, (HID, 256), 1)
    all_steps = bias_ref[...]
    column = lax.broadcasted_iota(jnp.int32, all_steps.shape, 1)
    extra = []
    for j in range(2):
        b = jnp.sum(jnp.where(column == 2 * rank_ref[0] + j, all_steps, 0.0), axis=1, keepdims=True) * 0.5
        b1 = b.astype(BF16).astype(F32)
        b2 = (b - b1).astype(BF16).astype(F32)
        b3 = b - b1 - b2
        extra.append(jnp.where(lane == 192, b1, jnp.where(lane == 193, b2, jnp.where(lane == 194, b3, 0.0))))
    for k in range(4):
        wk = lax.dot_general(w_ref[...], sel_ref[k], (((0,), (0,)), ((), ())), preferred_element_type=F32)
        for j in range(2):
            wbig_ref[j, k * HID:(k + 1) * HID, :] = (wk + extra[j]).astype(BF16)
    pick = lax.broadcasted_iota(jnp.int32, (16, C), 0) % C == lax.broadcasted_iota(jnp.int32, (16, C), 1)
    tall = jnp.dot(jnp.where(pick, 1.0, 0.0).astype(BF16), out_ref[...], preferred_element_type=F32)
    wide = jnp.concatenate([tall] * 4, 1)
    own = lax.broadcasted_iota(jnp.int32, (16, 512), 0) // C == lax.broadcasted_iota(jnp.int32, (16, 512), 1) // HID
    w2_ref[...] = jnp.where(own, wide, 0.0).astype(BF16)


INNER, OUTER = (1, 2), (0, 3)
CONV_SCRATCH = [
    pltpu.VMEM((2, 512, 256), BF16),
    pltpu.VMEM(((NX + 9) * 40, NY), F32),
    pltpu.VMEM((2, (NX + 10) * 48, NY), BF16),
    pltpu.VMEM(((NX + 16) * 16, NY), F32),
    pltpu.VMEM((8, 512, 256), BF16),
    pltpu.VMEM((8, 512, 256), BF16),
]


def clear(S, Q, HB):
    S[NX * 40:(NX + 9) * 40, :] = jnp.zeros((9 * 40, NY), F32)
    for i in range(2):
        Q[i, 0:48, :] = jnp.zeros((48, NY), BF16)
    HB[...] = jnp.zeros(HB.shape, BF16)


def conv_step(layer, pairs, wbig, w2_ref, put, S, Q, So, HA, HB, ready):
    for dp in sorted({2 * p + i for p in pairs for i in range(4)}):
        for c in range(C):
            S[pl.ds(dp * 4 + c, NX, stride=40), :] = layer(c, dp)
    lane = lax.broadcasted_iota(jnp.int32, (16, NY), 1)

    def prep(x):
        base = pl.multiple_of((x + 1) * 48, 16)
        for i, p in enumerate(pairs):
            v = S[pl.ds(pl.multiple_of(x * 40 + 8 * p, 8), 16), :]
            ve = [
                jnp.where(lane == 0, 0.0, pltpu.roll(v, 1, 1)),
                v,
                jnp.where(lane == NY - 1, 0.0, pltpu.roll(v, NY - 1, 1)),
            ]
            for e in range(3):
                Q[i, pl.ds(base + 16 * e, 16), :] = ve[e].astype(BF16)

    for x in range(9):
        prep(x)
    ready()
    ones = jnp.ones((16, 256), BF16)

    def first(t, hidden):
        for g in range(8):
            xq, i = 4 * t + g // 2, g % 2
            b0 = pl.multiple_of(xq * 192, 16)
            pa = Q[i, pl.ds(b0, 192), :]
            pb = Q[i, pl.ds(b0 + 96, 192), :]
            patch = jnp.concatenate([jnp.concatenate([pa, pb], 1), ones], 0)
            u = jnp.dot(wbig[:, 0:208], patch, preferred_element_type=F32)
            hidden[g] = (u + u * jnp.tanh(u)).astype(BF16)
            for k in range(2):
                prep(16 * t + 9 + 2 * g + k)
            yield

    def second(t, hidden):
        for g in range(8):
            xq, i = 4 * t + g // 2, g % 2
            r = jnp.dot(w2_ref[...], hidden[g], preferred_element_type=F32)
            for hh in range(2):
                for xx in range(2):
                    st = pl.multiple_of((xq * 4 + 16 + 2 * hh + xx) * 16, 8)
                    So[pl.ds(st + i * 8, 8), :] = r[xx * 8:xx * 8 + 8, hh * NY:hh * NY + NY]
            yield

    def body(i, carry):
        for _ in zip(first(2 * i, HA), second(2 * i - 1, HB)):
            pass
        for _ in zip(first(2 * i + 1, HB), second(2 * i, HA)):
            pass
        return carry

    lax.fori_loop(0, NX // 32, body, 0)
    for _ in second(NX // 16 - 1, HB):
        pass
    for i in range(2):
        for dd in range(2):
            for c in range(C):
                put(c, 2 * i + dd, So[pl.ds(256 + i * 8 + dd * 4 + c, NX, stride=16), :])


def convolve(state, pairs, halo, w2_ref, put, loads, scratch):
    wbig, S, Q, So, HA, HB = scratch
    clear(S, Q, HB)

    def layer(j, c, dp):
        if dp in (0, ND + 1):
            return halo[dp > 0][j, c].astype(F32)
        return state(j, c, dp - 1)

    for j in range(2):
        loads.wait(f"step{j}")
        conv_step(
            lambda c, dp: layer(j, c, dp), pairs, wbig.at[j], w2_ref, lambda c, i, v: put(j, c, i, v),
            S, Q, So, HA, HB, lambda: loads.wait("weights"),
        )


def increments(state, rank_ref, ts_ref, in_ref, out_ref, n_ref, g_ref, start, pay_ref, sums_refs):
    step, gain = gains(rank_ref, ts_ref)
    for p in range(4):
        for c in range(C):
            totals = []
            for dd in range(2):
                d = 2 * p + dd
                observed, count = guide_at(g_ref, d, c)
                total = start(c, d)
                for j in range(2):
                    drift = in_ref[j, c, d - 2] if p in INNER else out_ref[j, c, d if p == 0 else d - 4]
                    drift = drift + GUIDE_GAIN * (observed - count * state(j, c, d))
                    total = total + step[j] * drift + gain[j] * n_ref[j, c, d].astype(F32)
                    if j < len(sums_refs):
                        sums_refs[j][c, d] = total
                totals.append(total)
            encode(totals, lambda at, n, v: pay_ref.__setitem__((c, p, pl.ds(at, n), slice(None)), v))


def given(s_ref):
    return lambda j, c, d: s_ref[j, c, d]


def first_of(rank_ref, start_ref):
    keep = jnp.where(rank_ref[0] == 0, 1.0, 0.0)
    return lambda c, d: keep * start_ref[c, d]


def arrived(e_ref, start, sum_ref):
    def state(j, c, d):
        get = lambda at, n: e_ref[c, d // 2, pl.ds(at, n), :]
        entering = decode(get, d % 2, scale_of(get))
        return entering + (start(c, d) if j == 0 else sum_ref[c, d])

    return state


def inner1_kernel(s_hbm, wbig_hbm, w2_ref, o_ref, s, sems, *scratch):
    loads = Loads(
        sems, step0=[(s_hbm.at[0, :, 1:7], s.at[0])], weights=[(wbig_hbm, scratch[0])], step1=[(s_hbm.at[1, :, 1:7], s.at[1])]
    )
    put = lambda j, c, i, v: o_ref.__setitem__((j, c, i), v)
    convolve(lambda j, c, d: s[j, c, d - 1], INNER, None, w2_ref, put, loads, scratch)


def outer1_kernel(
    rank_ref, ts_ref, lo_ref, hi_ref, w2_ref, s_hbm, wbig_hbm, in_hbm_ref, n_hbm, own_hbm, other_hbm,
    pay_ref, sum_ref, s, in_ref, n_ref, g_ref, out_ref, sems, *scratch,
):
    layers = lambda j, lo, hi: (s_hbm.at[j, :, lo:hi], s.at[j, :, lo:hi])
    step = lambda j: [layers(j, 0, 3), layers(j, 5, 8)]
    loads = Loads(
        sems, step0=step(0), weights=[(wbig_hbm, scratch[0])], step1=step(1),
        late=[layers(0, 3, 5), layers(1, 3, 5), (n_hbm, n_ref), (own_hbm, g_ref.at[rank_ref[0] % 2]), (other_hbm, g_ref.at[1 - rank_ref[0] % 2]), (in_hbm_ref, in_ref)],
    )
    put = lambda j, c, i, v: out_ref.__setitem__((j, c, i), v)
    convolve(given(s), OUTER, (lo_ref, hi_ref), w2_ref, put, loads, scratch)
    loads.wait("late")
    start = first_of(rank_ref, s.at[0])
    increments(given(s), rank_ref, ts_ref, in_ref, out_ref, n_ref, g_ref, start, pay_ref, [sum_ref])


def gains(rank_ref, ts_ref):
    tm = rank_ref[0]
    step, gain = [], []
    for j in range(2):
        span = jnp.full((1, NY), ts_ref[2 * tm + j] - ts_ref[2 * tm + j + 1], jnp.int32).astype(F32) / TIME_SCALE
        step.append(span)
        gain.append(jnp.sqrt(span) * NOISE_COEF)
    return step, gain


def inner2_kernel(rank_ref, e_ref, traj_hbm, before_hbm, wbig_hbm, w2_ref, o_ref, traj, before, sems, *scratch):
    loads = Loads(
        sems, step0=[(traj_hbm.at[0, :, 1:7], traj.at[0, :, 1:7])], weights=[(wbig_hbm, scratch[0])],
        step1=[(before_hbm.at[:, 1:7], before.at[:, 1:7])],
    )
    state = arrived(e_ref, first_of(rank_ref, traj.at[0]), before)
    put = lambda j, c, i, v: o_ref.__setitem__((j, c, i), v)
    convolve(state, INNER, None, w2_ref, put, loads, scratch)


def outer2_kernel(
    rank_ref, ts_ref, e_ref, lo_ref, hi_ref, w2_ref, traj_hbm, before_hbm, wbig_hbm, in_hbm_ref, n_hbm, own_hbm, other_hbm,
    pay_ref, sum0_ref, sum1_ref, traj, before, in_ref, n_ref, g_ref, out_ref, sems, *scratch,
):
    loads = Loads(
        sems, step0=[(traj_hbm.at[0:1], traj)], weights=[(wbig_hbm, scratch[0])], step1=[(before_hbm, before)],
        late=[(n_hbm, n_ref), (own_hbm, g_ref.at[rank_ref[0] % 2]), (other_hbm, g_ref.at[1 - rank_ref[0] % 2]), (in_hbm_ref, in_ref)],
    )
    start = first_of(rank_ref, traj.at[0])
    state = arrived(e_ref, start, before)
    put = lambda j, c, i, v: out_ref.__setitem__((j, c, i), v)
    convolve(state, OUTER, (lo_ref, hi_ref), w2_ref, put, loads, scratch)
    loads.wait("late")
    increments(state, rank_ref, ts_ref, in_ref, out_ref, n_ref, g_ref, start, pay_ref, [sum0_ref, sum1_ref])


def edges_kernel(rank_ref, e_ref, start_ref, sum_ref, top_ref, bottom_ref):
    state = arrived(e_ref, first_of(rank_ref, start_ref.at[0]), sum_ref)
    for j in range(2):
        for c in range(C):
            top_ref[j, c] = state(j, c, 0).astype(BF16)
            bottom_ref[j, c] = state(j, c, ND - 1).astype(BF16)


def last_kernel(e_ref, sum0_ref, sum1_ref, o_ref):
    for c in range(C):
        get = lambda at, n: e_ref[c, pl.ds(at, n), :]
        scale = scale_of(get)
        for dd in range(2):
            entering = decode(get, dd, scale)
            o_ref[0, c, dd] = entering + sum0_ref[c, dd]
            o_ref[1, c, dd] = entering + sum1_ref[c, dd]


def last_states(entering, sum0, sum1):
    one = lambda: pl.BlockSpec((C, 2, NX, NY), lambda p: (0, p, 0, 0))
    return pl.pallas_call(
        last_kernel,
        grid=(4,),
        in_specs=[pl.BlockSpec((C, None, PAY, NY), lambda p: (0, p, 0, 0)), one(), one()],
        out_specs=pl.BlockSpec((2, C, 2, NX, NY), lambda p: (0, 0, p, 0, 0)),
        out_shape=shape(F32, 2, C, ND, NX, NY),
        compiler_params=params(16),
        name="last_states",
    )(entering, sum0, sum1)


def wells_kernel(rank_ref, rows_ref, *refs):
    o_ref, total_ref = refs[-2:]
    half, me_space = rank_ref[0] % 2, rank_ref[1]
    line = lax.broadcasted_iota(jnp.int32, (HID, ROWS), 0)
    column = lax.broadcasted_iota(jnp.int32, (2 * NY, ROWS), 0)
    for src in range(SPACE):
        owner = rows_ref[src, 0:1, :].astype(jnp.int32)
        cell = rows_ref[src, 1:2, :].astype(jnp.int32)
        here = jnp.logical_and(owner == me_space, (cell >> 15) == half)
        at_line = jnp.where(here, ((cell >> 13) & 3) * 32 + ((cell >> 7) & 31), -1)
        hit = jnp.where(line == at_line, 1.0, 0.0)
        pieces = [hit.astype(BF16)]
        for c in range(C):
            v = rows_ref[src, 2 + c:3 + c, :]
            v1 = v.astype(BF16).astype(F32)
            pieces += [(hit * v1).astype(BF16), (hit * (v - v1)).astype(BF16)]
        left = jnp.concatenate(pieces, 0)
        right = jnp.where(column == ((cell >> 12) & 1) * NY + (cell & 127), 1.0, 0.0).astype(BF16)
        part = lax.dot_general(left, right, (((1,), (1,)), ((), ())), preferred_element_type=F32)
        total_ref[...] = part if src == 0 else total_ref[...] + part
    for d in range(4):
        term = lambda k: jnp.concatenate(
            [total_ref[pl.ds(k * HID + 32 * d, 32), pl.ds(h * NY, NY)] for h in range(2)], 0
        )
        observed = [term(1 + 2 * c) + term(2 + 2 * c) for c in range(C)]
        power, factor = power_of(observed)
        for c in range(C):
            o_ref[d, c * NX:(c + 1) * NX, :] = jnp.round(observed[c] * factor).astype(jnp.int32).astype(I16)
        o_ref[d, C * NX:5 * NX, :] = term(0).astype(jnp.int32).astype(I16)
        o_ref[d, 5 * NX:GROWS, :] = jnp.broadcast_to(power, (16, NY)).astype(jnp.int32).astype(I16)


def wells(ranks, rows, *earlier):
    return pl.pallas_call(
        wells_kernel,
        grid=(1,),
        in_specs=[smem(), full(rows.shape)] + [pl.BlockSpec(memory_space=pl.ANY)] * len(earlier),
        out_specs=full((4, GROWS, NY)),
        out_shape=shape(I16, 4, GROWS, NY),
        scratch_shapes=[pltpu.VMEM((9 * HID, 2 * NY), F32)],
        compiler_params=params(24),
        name="wells",
    )(ranks, rows, *earlier)


def guide_at(g_ref, d, c):
    wide = lambda at, n: g_ref[d // 4, d % 4, pl.ds(at, n), :].astype(jnp.int32).astype(F32)
    return wide(c * NX, NX) * jnp.exp2(wide(5 * NX, 16)[0:1]), wide(C * NX, NX)


def power_of(planes):
    top = functools.reduce(jnp.maximum, [jnp.max(jnp.abs(v), axis=0, keepdims=True) for v in planes])
    power = jnp.ceil(jnp.log2(jnp.maximum(top, 1e-30) * (1.0 / 32000.0)))
    return power, jnp.exp2(-power)


def encode(planes, put):
    power, factor = power_of(planes)
    for i in range(2):
        put(i * NX, NX, jnp.round(planes[i] * factor).astype(jnp.int32).astype(I16))
    put(2 * NX, EXP, jnp.broadcast_to(power, (EXP, NY)).astype(jnp.int32).astype(I16))


def scale_of(get):
    return jnp.exp2(get(2 * NX, EXP).astype(jnp.int32).astype(F32)[0:1])


def decode(get, i, scale):
    return get(i * NX, NX).astype(jnp.int32).astype(F32) * scale


def scan_kernel(got_ref, o_ref):
    running = [jnp.zeros((NX, NY), F32) for _ in range(2)]
    for k in range(TM):
        encode(running, lambda at, n, v: o_ref.__setitem__((k, pl.ds(at, n), slice(None)), v))
        if k < TM - 1:
            get = lambda at, n: got_ref[k, pl.ds(at, n), :]
            scale = scale_of(get)
            running = [running[i] + decode(get, i, scale) for i in range(2)]


def prefix(payload):
    got = lax.all_to_all(payload.reshape(TM, PAY, NY), "tm", 0, 0, tiled=True)
    ahead = call(scan_kernel, "scan", 6, shape(I16, TM, PAY, NY), [], got)
    return lax.all_to_all(ahead, "tm", 0, 0, tiled=True).reshape(C, 4, PAY, NY)


def halos(top, bottom):
    lo = lax.ppermute(bottom, "space", [(i, i + 1) for i in range(SPACE - 1)])
    hi = lax.ppermute(top, "space", [(i + 1, i) for i in range(SPACE - 1)])
    return lo, hi


def time_bias(w_time, times):
    half_width = w_time.shape[1] // 2
    frequency = jnp.exp(-math.log(10000.0) * jnp.arange(half_width, dtype=F32) / half_width)
    angles = times.astype(F32)[None, :] * frequency[:, None]
    features = jnp.concatenate([jnp.sin(angles), jnp.cos(angles)], 0).astype(BF16)
    return jnp.dot(w_time, features, preferred_element_type=F32)


def per_device(trajectory, noise, timesteps, w_in, w_time, w_out, well_cells, well_owner, well_values):
    ranks = jnp.stack([lax.axis_index("tm"), lax.axis_index("space")]).astype(jnp.int32)
    bias = time_bias(w_time, timesteps[:-1])
    rows, top, bottom = pack(in_hbm(well_owner.T), in_hbm(well_cells[None]), in_hbm(well_values.T), in_hbm(trajectory))
    wbig, w2 = call(
        weights_kernel, "weights", 8, [shape(BF16, 2, 512, 256), shape(BF16, 16, 512)],
        [ranks], w_in.T, jnp.asarray(selection(), BF16), bias, w_out,
    )
    rows = lax.all_to_all(rows, "space", 0, 0, tiled=True)
    lo, hi = halos(top, bottom)

    half = shape(F32, 2, C, 4, NX, NY)
    whole = shape(F32, C, ND, NX, NY)
    coded = shape(I16, C, 4, PAY, NY)
    edge = shape(BF16, 2, C, NX, NY)
    vm = lambda *dims: pltpu.VMEM(dims, F32)
    six = vm(2, C, 6, NX, NY)
    sems = lambda n: pltpu.SemaphoreType.DMA((n,))
    s, wbig = Hbm(trajectory), Anywhere(wbig)
    guide = wells(ranks, rows, lo, hi, wbig.value)
    guide = [Anywhere(guide), Anywhere(lax.ppermute(guide, "tm", [(i, i ^ 1) for i in range(TM)]))]
    part = call(inner1_kernel, "inner1", 24, half, [], s, wbig, w2, scratch=[six, sems(3)] + CONV_SCRATCH)
    mine = [vm(*half.shape), pltpu.VMEM((2, C, ND, NX, NY), BF16), pltpu.VMEM((2, 4, GROWS, NY), I16), vm(*half.shape)]
    payload, sums = call(
        outer1_kernel, "outer1", 34, [coded, whole], [ranks, timesteps],
        lo, hi, w2, s, wbig, Anywhere(part), Hbm(noise), *guide,
        scratch=[vm(2, C, ND, NX, NY)] + mine + [sems(11)] + CONV_SCRATCH,
    )
    entering = prefix(payload)
    lo, hi = halos(*call(edges_kernel, "edges", 8, [edge, edge], [ranks], entering, First(trajectory), sums))
    sums = Anywhere(sums)
    part = call(
        inner2_kernel, "inner2", 24, half, [ranks], entering, s, sums, wbig, w2,
        scratch=[vm(1, C, ND, NX, NY), vm(C, ND, NX, NY), sems(3)] + CONV_SCRATCH,
    )
    payload, sum0, sum1 = call(
        outer2_kernel, "outer2", 36, [coded, whole, whole], [ranks, timesteps],
        entering, lo, hi, w2, s, sums, wbig, Anywhere(part), Hbm(noise), *guide,
        scratch=[
            vm(1, C, ND, NX, NY), vm(C, ND, NX, NY)] + mine + [sems(7)] + CONV_SCRATCH,
    )
    return last_states(prefix(payload), sum0, sum1)


def solution(mesh):
    return jax.shard_map(
        per_device,
        mesh=mesh,
        in_specs=(
            P("tm", None, "space", None, None),
            P("tm", None, "space", None, None),
            P(),
            P(),
            P(),
            P(),
            P("space"),
            P("space", None),
            P("space", None),
        ),
        out_specs=P("tm", None, "space", None, None),
        check_vma=False,
    )
```

```python
import functools
import math

import jax
import jax.numpy as jnp
import numpy as np
from jax import lax
from jax.experimental import pallas as pl
from jax.experimental.pallas import tpu as pltpu
from jax.sharding import PartitionSpec as P

F32, BF16, I16 = jnp.float32, jnp.bfloat16, jnp.int16
C, HID, ND, NX, NY = 4, 128, 8, 64, 128
TM, SPACE = 16, 8
ROWS = 1024
GUIDE_GAIN = 2.0
NOISE_COEF = 0.5
TIME_SCALE = 500.0
EXP = 8
PAY = 2 * NX + EXP
GROWS = 5 * NX + 16
MIB = 2**20


def params(mib):
    return pltpu.CompilerParams(vmem_limit_bytes=mib * MIB)


def smem():
    return pl.BlockSpec(memory_space=pltpu.SMEM)


def full(dims):
    return pl.BlockSpec(dims, lambda i: (0,) * len(dims), pipeline_mode=pl.Buffered(1))


def in_hbm(value):
    return pltpu.with_memory_space_constraint(value, pltpu.HBM)


class Hbm:
    def __init__(self, value):
        self.value = in_hbm(value)


class Anywhere:
    def __init__(self, value):
        self.value = value


class First:
    def __init__(self, value):
        self.value = in_hbm(value)


def spec_of(v):
    if isinstance(v, Hbm):
        return pl.BlockSpec(memory_space=pltpu.HBM)
    if isinstance(v, Anywhere):
        return pl.BlockSpec(memory_space=pl.ANY)
    if isinstance(v, First):
        dims = v.value.shape
        return pl.BlockSpec((1,) + dims[1:], lambda i: (0,) * len(dims), pipeline_mode=pl.Buffered(1))
    return full(v.shape)


def call(kernel, name, mib, out_shape, scalars, *args, scratch=()):
    return pl.pallas_call(
        kernel,
        grid=(1,),
        in_specs=[smem()] * len(scalars) + [spec_of(v) for v in args],
        out_specs=jax.tree.map(lambda v: full(v.shape), out_shape),
        out_shape=out_shape,
        scratch_shapes=list(scratch),
        compiler_params=params(mib),
        name=name,
    )(*scalars, *[v.value if isinstance(v, (Hbm, Anywhere, First)) else v for v in args])


class Loads:
    def __init__(self, sems, **groups):
        self.copies, at = {}, 0
        for name, pairs in groups.items():
            self.copies[name] = [pltpu.make_async_copy(src, dst, sems.at[at + i]) for i, (src, dst) in enumerate(pairs)]
            at += len(pairs)
        for copies in self.copies.values():
            for copy in copies:
                copy.start()

    def wait(self, name):
        for copy in self.copies.pop(name, []):
            copy.wait()


def shape(dtype, *dims):
    return jax.ShapeDtypeStruct(dims, dtype)


def selection():
    sel = np.zeros((4, 108, 256), np.float32)
    for xx in range(2):
        for dd in range(2):
            for a in range(3):
                for b in range(3):
                    for e in range(3):
                        for c in range(C):
                            sel[xx * 2 + dd, (9 * a + 3 * b + e) * C + c, (xx + b) * 48 + e * 16 + (dd + a) * 4 + c] = 0.5
    return sel


def pack_kernel(owner_hbm, cell_hbm, value_hbm, traj_hbm, rows_ref, top_ref, bottom_ref, owner, cell, value, first, last, sems):
    copies = [
        pltpu.make_async_copy(src, dst, sems.at[i])
        for i, (src, dst) in enumerate([
            (owner_hbm, owner), (cell_hbm, cell), (value_hbm, value),
            (traj_hbm.at[:, :, 0], first), (traj_hbm.at[:, :, ND - 1], last),
        ])
    ]
    for copy in copies:
        copy.start()
    for copy in copies:
        copy.wait()
    rows = jnp.concatenate(
        [owner[...].astype(F32), cell[...].astype(F32), value[...], jnp.zeros((2, ROWS), F32)], 0
    )
    for k in range(SPACE):
        rows_ref[k] = rows
    top_ref[...] = first[...].astype(BF16)
    bottom_ref[...] = last[...].astype(BF16)


def pack(owner, cells, values, trajectory):
    edge = shape(BF16, 2, C, NX, NY)
    out_shape = [shape(F32, SPACE, 8, ROWS), edge, edge]
    layer = pltpu.VMEM((2, C, NX, NY), F32)
    return pl.pallas_call(
        pack_kernel,
        grid=(1,),
        in_specs=[pl.BlockSpec(memory_space=pltpu.HBM)] * 4,
        out_specs=[full(v.shape) for v in out_shape],
        out_shape=out_shape,
        scratch_shapes=[
            pltpu.VMEM((1, ROWS), jnp.int32), pltpu.VMEM((1, ROWS), jnp.int32), pltpu.VMEM((C, ROWS), F32),
            layer, layer, pltpu.SemaphoreType.DMA((5,)),
        ],
        compiler_params=params(8),
        name="pack",
    )(owner, cells, values, trajectory)


def weights_kernel(rank_ref, w_ref, sel_ref, bias_ref, out_ref, wbig_ref, w2_ref):
    lane = lax.broadcasted_iota(jnp.int32, (HID, 256), 1)
    all_steps = bias_ref[...]
    column = lax.broadcasted_iota(jnp.int32, all_steps.shape, 1)
    extra = []
    for j in range(2):
        b = jnp.sum(jnp.where(column == 2 * rank_ref[0] + j, all_steps, 0.0), axis=1, keepdims=True) * 0.5
        b1 = b.astype(BF16).astype(F32)
        b2 = (b - b1).astype(BF16).astype(F32)
        b3 = b - b1 - b2
        extra.append(jnp.where(lane == 192, b1, jnp.where(lane == 193, b2, jnp.where(lane == 194, b3, 0.0))))
    for k in range(4):
        wk = lax.dot_general(w_ref[...], sel_ref[k], (((0,), (0,)), ((), ())), preferred_element_type=F32)
        for j in range(2):
            wbig_ref[j, k * HID:(k + 1) * HID, :] = (wk + extra[j]).astype(BF16)
    pick = lax.broadcasted_iota(jnp.int32, (16, C), 0) % C == lax.broadcasted_iota(jnp.int32, (16, C), 1)
    tall = jnp.dot(jnp.where(pick, 1.0, 0.0).astype(BF16), out_ref[...], preferred_element_type=F32)
    wide = jnp.concatenate([tall] * 4, 1)
    own = lax.broadcasted_iota(jnp.int32, (16, 512), 0) // C == lax.broadcasted_iota(jnp.int32, (16, 512), 1) // HID
    w2_ref[...] = jnp.where(own, wide, 0.0).astype(BF16)


INNER, OUTER = (1, 2), (0, 3)
CONV_SCRATCH = [
    pltpu.VMEM((2, 512, 256), BF16),
    pltpu.VMEM(((NX + 9) * 40, NY), F32),
    pltpu.VMEM((2, (NX + 2) * 48, NY), BF16),
    pltpu.VMEM((NX * 16, NY), F32),
    pltpu.VMEM((8, 512, 256), BF16),
    pltpu.VMEM((8, 512, 256), BF16),
]


def convolve(state, pairs, halo, w2_ref, put, loads, scratch):
    wbig, S, Q, So, HA, HB = scratch
    S[NX * 40:(NX + 9) * 40, :] = jnp.zeros((9 * 40, NY), F32)
    for i in range(2):
        Q[i, 0:48, :] = jnp.zeros((48, NY), BF16)
    lane = lax.broadcasted_iota(jnp.int32, (16, NY), 1)
    ones = jnp.ones((16, 256), BF16)

    def fill(j):
        for dp in sorted({2 * p + i for p in pairs for i in range(4)}):
            for c in range(C):
                edge = dp in (0, ND + 1)
                v = halo[dp > 0][j, c].astype(F32) if edge else state(j, c, dp - 1)
                S[pl.ds(dp * 4 + c, NX, stride=40), :] = v

    def prep(x):
        base = (x + 1) * 48
        for i, p in enumerate(pairs):
            v = S[x * 40 + 8 * p:x * 40 + 8 * p + 16, :]
            ve = [
                jnp.where(lane == 0, 0.0, pltpu.roll(v, 1, 1)),
                v,
                jnp.where(lane == NY - 1, 0.0, pltpu.roll(v, NY - 1, 1)),
            ]
            for e in range(3):
                Q[i, base + 16 * e:base + 16 * e + 16, :] = ve[e].astype(BF16)

    def first(j, t, g, hidden):
        xq, i = 4 * t + g // 2, g % 2
        pa = Q[i, xq * 192:xq * 192 + 192, :]
        pb = Q[i, xq * 192 + 96:xq * 192 + 288, :]
        patch = jnp.concatenate([jnp.concatenate([pa, pb], 1), ones], 0)
        u = jnp.dot(wbig[j, :, 0:208], patch, preferred_element_type=F32)
        hidden[g] = (u + u * jnp.tanh(u)).astype(BF16)
        for k in range(2):
            if 16 * t + 9 + 2 * g + k <= NX:
                prep(16 * t + 9 + 2 * g + k)

    def second(t, g, hidden):
        xq, i = 4 * t + g // 2, g % 2
        r = jnp.dot(w2_ref[...], hidden[g], preferred_element_type=F32)
        for hh in range(2):
            for xx in range(2):
                st = (xq * 4 + 2 * hh + xx) * 16 + i * 8
                So[st:st + 8, :] = r[xx * 8:xx * 8 + 8, hh * NY:hh * NY + NY]

    def finish(j):
        for i in range(2):
            for dd in range(2):
                for c in range(C):
                    put(j, c, 2 * i + dd, So[pl.ds(i * 8 + dd * 4 + c, NX, stride=16), :])

    blocks = NX // 16
    behind = None
    for j in range(2):
        loads.wait(f"step{j}")
        fill(j)
        for x in range(9):
            prep(x)
        loads.wait("weights")
        for t in range(blocks):
            hidden = (HA, HB)[t % 2]
            for g in range(8):
                first(j, t, g, hidden)
                if behind:
                    second(behind[1], g, behind[2])
            if behind and behind[1] == blocks - 1:
                finish(behind[0])
            behind = (j, t, hidden)
    for g in range(8):
        second(behind[1], g, behind[2])
    finish(behind[0])


def increments(state, rank_ref, ts_ref, in_ref, out_ref, n_ref, g_ref, start, pay_ref, sums_refs):
    step, gain = gains(rank_ref, ts_ref)
    for p in range(4):
        for c in range(C):
            totals = []
            for dd in range(2):
                d = 2 * p + dd
                observed, count = guide_at(g_ref, d, c)
                total = start(c, d)
                for j in range(2):
                    drift = in_ref[j, c, d - 2] if p in INNER else out_ref[j, c, d if p == 0 else d - 4]
                    drift = drift + GUIDE_GAIN * (observed - count * state(j, c, d))
                    total = total + step[j] * drift + gain[j] * n_ref[j, c, d].astype(F32)
                    if j < len(sums_refs):
                        sums_refs[j][c, d] = total
                totals.append(total)
            encode(totals, lambda at, n, v: pay_ref.__setitem__((c, p, pl.ds(at, n), slice(None)), v))


def given(s_ref):
    return lambda j, c, d: s_ref[j, c, d]


def first_of(rank_ref, start_ref):
    keep = jnp.where(rank_ref[0] == 0, 1.0, 0.0)
    return lambda c, d: keep * start_ref[c, d]


def arrived(e_ref, start, sum_ref):
    def state(j, c, d):
        get = lambda at, n: e_ref[c, d // 2, pl.ds(at, n), :]
        entering = decode(get, d % 2, scale_of(get))
        return entering + (start(c, d) if j == 0 else sum_ref[c, d])

    return state


def inner1_kernel(s_hbm, wbig_hbm, w2_ref, o_ref, s, sems, *scratch):
    loads = Loads(
        sems, step0=[(s_hbm.at[0, :, 1:7], s.at[0])], weights=[(wbig_hbm, scratch[0])], step1=[(s_hbm.at[1, :, 1:7], s.at[1])]
    )
    put = lambda j, c, i, v: o_ref.__setitem__((j, c, i), v)
    convolve(lambda j, c, d: s[j, c, d - 1], INNER, None, w2_ref, put, loads, scratch)


def outer1_kernel(
    rank_ref, ts_ref, lo_ref, hi_ref, w2_ref, s_hbm, wbig_hbm, in_hbm_ref, n_hbm, own_hbm, other_hbm,
    pay_ref, sum_ref, s, in_ref, n_ref, g_ref, out_ref, sems, *scratch,
):
    layers = lambda j, lo, hi: (s_hbm.at[j, :, lo:hi], s.at[j, :, lo:hi])
    step = lambda j: [layers(j, 0, 3), layers(j, 5, 8)]
    loads = Loads(
        sems, step0=step(0), weights=[(wbig_hbm, scratch[0])], step1=step(1),
        late=[layers(0, 3, 5), layers(1, 3, 5), (n_hbm, n_ref), (own_hbm, g_ref.at[rank_ref[0] % 2]), (other_hbm, g_ref.at[1 - rank_ref[0] % 2]), (in_hbm_ref, in_ref)],
    )
    put = lambda j, c, i, v: out_ref.__setitem__((j, c, i), v)
    convolve(given(s), OUTER, (lo_ref, hi_ref), w2_ref, put, loads, scratch)
    loads.wait("late")
    start = first_of(rank_ref, s.at[0])
    increments(given(s), rank_ref, ts_ref, in_ref, out_ref, n_ref, g_ref, start, pay_ref, [sum_ref])


def gains(rank_ref, ts_ref):
    tm = rank_ref[0]
    step, gain = [], []
    for j in range(2):
        span = jnp.full((1, NY), ts_ref[2 * tm + j] - ts_ref[2 * tm + j + 1], jnp.int32).astype(F32) / TIME_SCALE
        step.append(span)
        gain.append(jnp.sqrt(span) * NOISE_COEF)
    return step, gain


def inner2_kernel(rank_ref, e_ref, traj_hbm, before_hbm, wbig_hbm, w2_ref, o_ref, traj, before, sems, *scratch):
    loads = Loads(
        sems, step0=[(traj_hbm.at[0, :, 1:7], traj.at[0, :, 1:7])], weights=[(wbig_hbm, scratch[0])],
        step1=[(before_hbm.at[:, 1:7], before.at[:, 1:7])],
    )
    state = arrived(e_ref, first_of(rank_ref, traj.at[0]), before)
    put = lambda j, c, i, v: o_ref.__setitem__((j, c, i), v)
    convolve(state, INNER, None, w2_ref, put, loads, scratch)


def outer2_kernel(
    rank_ref, ts_ref, e_ref, lo_ref, hi_ref, w2_ref, traj_hbm, before_hbm, wbig_hbm, in_hbm_ref, n_hbm, own_hbm, other_hbm,
    pay_ref, sum0_ref, sum1_ref, traj, before, in_ref, n_ref, g_ref, out_ref, sems, *scratch,
):
    loads = Loads(
        sems, step0=[(traj_hbm.at[0:1], traj)], weights=[(wbig_hbm, scratch[0])], step1=[(before_hbm, before)],
        late=[(n_hbm, n_ref), (own_hbm, g_ref.at[rank_ref[0] % 2]), (other_hbm, g_ref.at[1 - rank_ref[0] % 2]), (in_hbm_ref, in_ref)],
    )
    start = first_of(rank_ref, traj.at[0])
    state = arrived(e_ref, start, before)
    put = lambda j, c, i, v: out_ref.__setitem__((j, c, i), v)
    convolve(state, OUTER, (lo_ref, hi_ref), w2_ref, put, loads, scratch)
    loads.wait("late")
    increments(state, rank_ref, ts_ref, in_ref, out_ref, n_ref, g_ref, start, pay_ref, [sum0_ref, sum1_ref])


def edges_kernel(rank_ref, e0_ref, e7_ref, start0_ref, start7_ref, sum0_ref, sum7_ref, top_ref, bottom_ref):
    keep = jnp.where(rank_ref[0] == 0, 1.0, 0.0)
    for e_ref, start_ref, sum_ref, i, o_ref in (
        (e0_ref, start0_ref, sum0_ref, 0, top_ref), (e7_ref, start7_ref, sum7_ref, 1, bottom_ref)
    ):
        for c in range(C):
            get = lambda at, n: e_ref[c, pl.ds(at, n), :]
            entering = decode(get, i, scale_of(get))
            o_ref[0, c] = (entering + keep * start_ref[c]).astype(BF16)
            o_ref[1, c] = (entering + sum_ref[c]).astype(BF16)


def edges(ranks, entering, trajectory, sums):
    edge = shape(BF16, 2, C, NX, NY)
    pair = lambda p: pl.BlockSpec((C, None, PAY, NY), lambda i: (0, p, 0, 0), pipeline_mode=pl.Buffered(1))
    first = lambda d: pl.BlockSpec((None, C, None, NX, NY), lambda i: (0, 0, d, 0, 0), pipeline_mode=pl.Buffered(1))
    layer = lambda d: pl.BlockSpec((C, None, NX, NY), lambda i: (0, d, 0, 0), pipeline_mode=pl.Buffered(1))
    last = ND - 1
    return pl.pallas_call(
        edges_kernel,
        grid=(1,),
        in_specs=[smem(), pair(0), pair(3), first(0), first(last), layer(0), layer(last)],
        out_specs=[full(edge.shape)] * 2,
        out_shape=[edge, edge],
        compiler_params=params(8),
        name="edges",
    )(ranks, entering, entering, trajectory, trajectory, sums, sums)


def last_kernel(e_ref, sum0_ref, sum1_ref, o_ref):
    for c in range(C):
        get = lambda at, n: e_ref[c, pl.ds(at, n), :]
        scale = scale_of(get)
        for dd in range(2):
            entering = decode(get, dd, scale)
            o_ref[0, c, dd] = entering + sum0_ref[c, dd]
            o_ref[1, c, dd] = entering + sum1_ref[c, dd]


def last_states(entering, sum0, sum1):
    one = lambda: pl.BlockSpec((C, 2, NX, NY), lambda p: (0, p, 0, 0))
    return pl.pallas_call(
        last_kernel,
        grid=(4,),
        in_specs=[pl.BlockSpec((C, None, PAY, NY), lambda p: (0, p, 0, 0)), one(), one()],
        out_specs=pl.BlockSpec((2, C, 2, NX, NY), lambda p: (0, 0, p, 0, 0)),
        out_shape=shape(F32, 2, C, ND, NX, NY),
        compiler_params=params(16),
        name="last_states",
    )(entering, sum0, sum1)


def wells_kernel(rank_ref, rows_ref, *refs):
    o_ref, total_ref = refs[-2:]
    half, me_space = rank_ref[0] % 2, rank_ref[1]
    line = lax.broadcasted_iota(jnp.int32, (HID, ROWS), 0)
    column = lax.broadcasted_iota(jnp.int32, (2 * NY, ROWS), 0)
    for src in range(SPACE):
        owner = rows_ref[src, 0:1, :].astype(jnp.int32)
        cell = rows_ref[src, 1:2, :].astype(jnp.int32)
        here = jnp.logical_and(owner == me_space, (cell >> 15) == half)
        at_line = jnp.where(here, ((cell >> 13) & 3) * 32 + ((cell >> 7) & 31), -1)
        hit = jnp.where(line == at_line, 1.0, 0.0)
        pieces = [hit.astype(BF16)]
        for c in range(C):
            v = rows_ref[src, 2 + c:3 + c, :]
            v1 = v.astype(BF16).astype(F32)
            pieces += [(hit * v1).astype(BF16), (hit * (v - v1)).astype(BF16)]
        left = jnp.concatenate(pieces, 0)
        right = jnp.where(column == ((cell >> 12) & 1) * NY + (cell & 127), 1.0, 0.0).astype(BF16)
        part = lax.dot_general(left, right, (((1,), (1,)), ((), ())), preferred_element_type=F32)
        total_ref[...] = part if src == 0 else total_ref[...] + part
    for d in range(4):
        term = lambda k: jnp.concatenate(
            [total_ref[pl.ds(k * HID + 32 * d, 32), pl.ds(h * NY, NY)] for h in range(2)], 0
        )
        observed = [term(1 + 2 * c) + term(2 + 2 * c) for c in range(C)]
        power, factor = power_of(observed)
        for c in range(C):
            o_ref[d, c * NX:(c + 1) * NX, :] = jnp.round(observed[c] * factor).astype(jnp.int32).astype(I16)
        o_ref[d, C * NX:5 * NX, :] = term(0).astype(jnp.int32).astype(I16)
        o_ref[d, 5 * NX:GROWS, :] = jnp.broadcast_to(power, (16, NY)).astype(jnp.int32).astype(I16)


def wells(ranks, rows, *earlier):
    return pl.pallas_call(
        wells_kernel,
        grid=(1,),
        in_specs=[smem(), full(rows.shape)] + [pl.BlockSpec(memory_space=pl.ANY)] * len(earlier),
        out_specs=full((4, GROWS, NY)),
        out_shape=shape(I16, 4, GROWS, NY),
        scratch_shapes=[pltpu.VMEM((9 * HID, 2 * NY), F32)],
        compiler_params=params(24),
        name="wells",
    )(ranks, rows, *earlier)


def guide_at(g_ref, d, c):
    wide = lambda at, n: g_ref[d // 4, d % 4, pl.ds(at, n), :].astype(jnp.int32).astype(F32)
    return wide(c * NX, NX) * jnp.exp2(wide(5 * NX, 16)[0:1]), wide(C * NX, NX)


def power_of(planes):
    top = functools.reduce(jnp.maximum, [jnp.max(jnp.abs(v), axis=0, keepdims=True) for v in planes])
    power = jnp.ceil(jnp.log2(jnp.maximum(top, 1e-30) * (1.0 / 32000.0)))
    return power, jnp.exp2(-power)


def encode(planes, put):
    power, factor = power_of(planes)
    for i in range(2):
        put(i * NX, NX, jnp.round(planes[i] * factor).astype(jnp.int32).astype(I16))
    put(2 * NX, EXP, jnp.broadcast_to(power, (EXP, NY)).astype(jnp.int32).astype(I16))


def scale_of(get):
    return jnp.exp2(get(2 * NX, EXP).astype(jnp.int32).astype(F32)[0:1])


def decode(get, i, scale):
    return get(i * NX, NX).astype(jnp.int32).astype(F32) * scale


def scan_kernel(got_ref, o_ref):
    running = [jnp.zeros((NX, NY), F32) for _ in range(2)]
    for k in range(TM):
        encode(running, lambda at, n, v: o_ref.__setitem__((k, pl.ds(at, n), slice(None)), v))
        if k < TM - 1:
            get = lambda at, n: got_ref[k, pl.ds(at, n), :]
            scale = scale_of(get)
            running = [running[i] + decode(get, i, scale) for i in range(2)]


def prefix(payload):
    got = lax.all_to_all(payload.reshape(TM, PAY, NY), "tm", 0, 0, tiled=True)
    ahead = call(scan_kernel, "scan", 6, shape(I16, TM, PAY, NY), [], got)
    return lax.all_to_all(ahead, "tm", 0, 0, tiled=True).reshape(C, 4, PAY, NY)


def halos(top, bottom):
    lo = lax.ppermute(bottom, "space", [(i, i + 1) for i in range(SPACE - 1)])
    hi = lax.ppermute(top, "space", [(i + 1, i) for i in range(SPACE - 1)])
    return lo, hi


def time_bias(w_time, times):
    half_width = w_time.shape[1] // 2
    frequency = jnp.exp(-math.log(10000.0) * jnp.arange(half_width, dtype=F32) / half_width)
    angles = times.astype(F32)[None, :] * frequency[:, None]
    features = jnp.concatenate([jnp.sin(angles), jnp.cos(angles)], 0).astype(BF16)
    return jnp.dot(w_time, features, preferred_element_type=F32)


def per_device(trajectory, noise, timesteps, w_in, w_time, w_out, well_cells, well_owner, well_values):
    ranks = jnp.stack([lax.axis_index("tm"), lax.axis_index("space")]).astype(jnp.int32)
    bias = time_bias(w_time, timesteps[:-1])
    rows, top, bottom = pack(in_hbm(well_owner.T), in_hbm(well_cells[None]), in_hbm(well_values.T), in_hbm(trajectory))
    wbig, w2 = call(
        weights_kernel, "weights", 8, [shape(BF16, 2, 512, 256), shape(BF16, 16, 512)],
        [ranks], w_in.T, jnp.asarray(selection(), BF16), bias, w_out,
    )
    rows = lax.all_to_all(rows, "space", 0, 0, tiled=True)
    lo, hi = halos(top, bottom)

    half = shape(F32, 2, C, 4, NX, NY)
    whole = shape(F32, C, ND, NX, NY)
    coded = shape(I16, C, 4, PAY, NY)
    edge = shape(BF16, 2, C, NX, NY)
    vm = lambda *dims: pltpu.VMEM(dims, F32)
    six = vm(2, C, 6, NX, NY)
    sems = lambda n: pltpu.SemaphoreType.DMA((n,))
    s, wbig = Hbm(trajectory), Anywhere(wbig)
    guide = wells(ranks, rows, lo, hi, wbig.value)
    guide = [Anywhere(guide), Anywhere(lax.ppermute(guide, "tm", [(i, i ^ 1) for i in range(TM)]))]
    part = call(inner1_kernel, "inner1", 24, half, [], s, wbig, w2, scratch=[six, sems(3)] + CONV_SCRATCH)
    mine = [vm(*half.shape), pltpu.VMEM((2, C, ND, NX, NY), BF16), pltpu.VMEM((2, 4, GROWS, NY), I16), vm(*half.shape)]
    payload, sums = call(
        outer1_kernel, "outer1", 34, [coded, whole], [ranks, timesteps],
        lo, hi, w2, s, wbig, Anywhere(part), Hbm(noise), *guide,
        scratch=[vm(2, C, ND, NX, NY)] + mine + [sems(11)] + CONV_SCRATCH,
    )
    entering = prefix(payload)
    lo, hi = halos(*edges(ranks, entering, s.value, sums))
    sums = Anywhere(sums)
    part = call(
        inner2_kernel, "inner2", 24, half, [ranks], entering, s, sums, wbig, w2,
        scratch=[vm(1, C, ND, NX, NY), vm(C, ND, NX, NY), sems(3)] + CONV_SCRATCH,
    )
    payload, sum0, sum1 = call(
        outer2_kernel, "outer2", 36, [coded, whole, whole], [ranks, timesteps],
        entering, lo, hi, w2, s, sums, wbig, Anywhere(part), Hbm(noise), *guide,
        scratch=[
            vm(1, C, ND, NX, NY), vm(C, ND, NX, NY)] + mine + [sems(7)] + CONV_SCRATCH,
    )
    return last_states(prefix(payload), sum0, sum1)


def solution(mesh):
    return jax.shard_map(
        per_device,
        mesh=mesh,
        in_specs=(
            P("tm", None, "space", None, None),
            P("tm", None, "space", None, None),
            P(),
            P(),
            P(),
            P(),
            P("space"),
            P("space", None),
            P("space", None),
        ),
        out_specs=P("tm", None, "space", None, None),
        check_vma=False,
    )
```
